256 devices in a mesh: flow: 8 (over x, core), cross: 8 (over z), depth: 4 (over y).
Axes of the slice: x: 4, y: 4, z: 8, core: 2. Of those that a mesh axis runs over, the one named last changes fastest.
Arguments:
- fluid_offsets: float32 [3, 8, 32, 16, 128], P(None, 'flow', 'cross', 'depth'), may hold values from 0 to 1
- source: float32 [8, 32, 16, 128], P('flow', 'cross', 'depth'), may hold values from -6 to 6
- marker_offsets: float32 [4096, 16, 3, 128], P(('flow', 'cross', 'depth')), may hold values from 0 to 1
- marker_normals: float32 [4096, 16, 3, 128], P(('flow', 'cross', 'depth')), may hold values from -6 to 6
- dest_tile: int32 [4096, 16, 1], P(('flow', 'cross', 'depth')), may hold values from 0 to 63; in each aligned block of 256 rows (0 to 255, 256 to 511, ..., all dimensions but the last counted through in order) at most 8 rows name the same one
- cell_index: int32 [4096, 16], P(('flow', 'cross', 'depth')), may hold values from 0 to 15
- grain_velocity: float32 [4096, 3], P(('flow', 'cross', 'depth')), may hold values from -6 to 6
- grain_mass: float32 [4096], P(('flow', 'cross', 'depth')), may hold values from 0.5 to 4
Outputs:
- pressure: float32 [8, 32, 16, 128], P('flow', 'cross', 'depth')
- velocity_out: float32 [4096, 3], P(('flow', 'cross', 'depth'))
The draws below stay inside these ranges and needn't reach their ends.
Inputs may be any that keep to these rules, and one draw needn't show every extreme that they name: `dest_tile`: in the rows of one device at most 8 marker blocks name the same tile.
All inputs are finite; a program needn't handle non-finite values.
Results may differ from the reference program's by a relative error of at most 0.0003.
Values sent between devices are 32-bit elements; how exact they have to be, the bound alone decides.
No kernel may reach another device: no remote copies, remote signals or barrier semaphores. Data moves between devices by JAX's collectives and lax.ppermute only.
A program may use at most 64 MiB of HBM per device.

```python
import math
import jax
import jax.numpy as jnp
import numpy as np
from jax import lax

CX = 1
CY = 4
CZ = 4
G_DEV = 16
MB = 16
ITERS = 4
STEPS = 2
CELLS = 16
NX = 8
NY = 32
NZ = 16
GRAINS = 4096
CAP = 8
N_FLOW = 8
N_CROSS = 8
N_DEPTH = 4


def touch_ends(values, stream_key, least, high):
    dims = values.shape
    spot = [jax.random.randint(jax.random.fold_in(stream_key, axis), (), 0, dims[axis]) for axis in range(len(dims))]
    values = values.at[tuple(spot)].set(least)
    longest = dims.index(max(dims))
    spot[longest] = (spot[longest] + 1) % dims[longest]
    return values.at[tuple(spot)].set(high)


def block_levels(stream_key, shape, split, low, high):
    gain, own = 1.0, jax.random.fold_in(stream_key, 6)
    for position, parts in split:
        draws = jnp.exp(jax.random.uniform(jax.random.fold_in(own, position), (parts,), jnp.float32, low / len(split), high / len(split)))
        gain = gain * jnp.repeat(draws, shape[position] // parts).reshape([-1 if axis == position else 1 for axis in range(len(shape))])
    return gain


def assign_block(own_key, own, number, rows, amount, top, limit, slope):
    order = jax.random.permutation(own_key, amount)
    packed, ordinary = load_shares(amount, rows * top, limit, slope, True), load_shares(amount, rows * top, limit, slope, False)
    places = jnp.arange(amount)

    def named(sizes, offset_by):
        used = int((sizes > 0).sum())
        fixed = max(1, used // 4)
        moved = fixed + (places - fixed + offset_by * (used - fixed)) % max(1, amount - fixed)
        return jnp.zeros((amount,), jnp.int32).at[order[jnp.where(places < fixed, places, moved)]].set(jnp.asarray(sizes, jnp.int32))

    sizes = jnp.where(number % 4 == 0, named(packed, number // 4), named(ordinary, number - number // 4 - 1))
    mixed = jax.random.permutation(jax.random.fold_in(own, 3), amount)
    source_of, receiver = mixed[0:amount // 2 * 2:2], mixed[1:amount // 2 * 2:2]
    margin = jnp.minimum(sizes[source_of] - 1, limit - sizes[receiver]) // 2
    margin = jnp.where((source_of == order[0]) | (receiver == order[0]) | (sizes[receiver] == 0), 0, jnp.maximum(margin, 0))
    moved = jax.random.randint(jax.random.fold_in(own, 4), (amount // 2,), 0, 1 << 20) % (margin + 1)
    sizes = sizes.at[source_of].add(-moved).at[receiver].add(moved)
    items = jnp.searchsorted(jnp.cumsum(sizes), jnp.arange(rows * top), side="right").astype(jnp.int32)
    grid = items.reshape(top, rows).T
    grid = grid[jax.random.permutation(jax.random.fold_in(own, 1), rows)]
    offset_by = jax.random.randint(jax.random.fold_in(own, 2), (rows, 1), 0, top)
    return jnp.take_along_axis(grid, (jnp.arange(top)[None, :] + offset_by) % top, axis=1)


def load_shares(number_of, total, bound, skew, full):
    portions = [(1 << 20) // math.isqrt(grade ** skew) + 1 for grade in range(1, number_of + 1)]
    largest = bound if full else min(bound, max(-(-total // number_of), total * portions[0] // sum(portions)))
    least = 1 if total - largest >= number_of - 1 else 0
    given, spare = [largest] + [least] * (number_of - 1), total - largest - least * (number_of - 1)
    while spare > 0:
        movable = [i for i in range(1, number_of) if given[i] < largest] or [i for i in range(1, number_of) if given[i] < bound]
        whole, budget = sum([portions[i] for i in movable]), spare
        for i in movable:
            extra = min(bound - given[i], max(1, budget * portions[i] // whole), spare)
            given[i] = given[i] + extra
            spare = spare - extra
    return np.array(given)


def centred(own_key, dims, spread, reach, split=(), kind=jnp.bfloat16):
    drawn = spread * jax.random.normal(own_key, dims, jnp.float32)
    if split:
        drawn = drawn * block_levels(own_key, dims, split, -0.22, 0.18)
    return jnp.clip(drawn, -reach, reach).astype(kind)


def setup_inputs(seed: int = 0) -> dict:
    arg_keys = jax.random.split(jax.random.key(seed), 9)
    fluid_offsets = jnp.clip(1.0 * jax.random.uniform(arg_keys[0], (3, NX, NY, NZ, 128), jnp.float32) ** block_levels(arg_keys[0], (3, NX, NY, NZ, 128), ((1, 8), (2, 8), (3, 4)), -0.2, 0.2), 0.0, 1.0)
    source = centred(arg_keys[1], (NX, NY, NZ, 128), 1.0, 6.0, ((0, 8), (1, 8), (2, 4)), jnp.float32)
    marker_offsets = jnp.clip(1.0 * jax.random.uniform(arg_keys[2], (GRAINS, MB, 3, 128), jnp.float32) ** block_levels(arg_keys[2], (GRAINS, MB, 3, 128), ((0, 256),), -0.2, 0.2), 0.0, 1.0)
    marker_normals = centred(arg_keys[3], (GRAINS, MB, 3, 128), 1.0, 6.0, ((0, 256),), jnp.float32)
    dest_tile_keys = jax.random.split(jax.random.fold_in(arg_keys[4], 1), GRAINS * MB // (G_DEV * MB))
    dest_tile_turns = jax.random.permutation(jax.random.fold_in(arg_keys[4], 3), GRAINS * MB // (G_DEV * MB))
    dest_tile = jax.vmap(lambda own, number: assign_block(jax.random.fold_in(arg_keys[4], 2), own, number, G_DEV * MB, N_FLOW * N_CROSS, 1, CAP, 2))(dest_tile_keys, dest_tile_turns).reshape((GRAINS, MB, 1))
    cell_index = touch_ends(jax.random.randint(arg_keys[5], (GRAINS, MB), 0, CELLS), jax.random.fold_in(arg_keys[5], 1), 0, CELLS - 1).astype(jnp.int32)
    grain_velocity = centred(arg_keys[6], (GRAINS, 3), 1.0, 6.0, ((0, 256),), jnp.float32)
    grain_mass = jnp.clip(jnp.exp(math.log(4.0) - 2.0794415 * jax.random.uniform(arg_keys[7], (GRAINS,), jnp.float32) ** block_levels(arg_keys[7], (GRAINS,), ((0, 256),), -0.2, 0.2)), 0.5, 4.0)
    return {"fluid_offsets": fluid_offsets, "source": source, "marker_offsets": marker_offsets, "marker_normals": marker_normals, "dest_tile": dest_tile, "cell_index": cell_index, "grain_velocity": grain_velocity, "grain_mass": grain_mass}


NEIGHBOURS = ((0, 0, 0), (1, 0, 0), (-1, 0, 0), (0, 1, 0), (0, -1, 0), (0, 0, 1), (0, 0, -1))
STIFFEN = 0.5
STEP_TIME = 0.05
PER_PARTICLE = 1.0 / 128.0


def pair_kernel(own_off, near_off, offset, values):
    total = None
    for component in range(3):
        gap = (near_off[component] + float(offset[component]))[..., None, :] - own_off[component][..., :, None]
        total = gap * gap if total is None else total + gap * gap
    weight = jnp.exp(-total) * PER_PARTICLE
    return jnp.sum(weight * values[..., None, :], axis=-1)


def marker_weights(fluid_rows, positions):
    total = None
    for component in range(3):
        gap = fluid_rows[:, component, :, None] - positions[:, component, None, :]
        total = gap * gap if total is None else total + gap * gap
    return jnp.exp(-total) * PER_PARTICLE


def weighted(fluid_offsets, field):
    def one_slab(slab_index):
        own_off = lax.dynamic_index_in_dim(fluid_offsets, slab_index, 1, keepdims=False)
        total = jnp.zeros(field.shape[1:], jnp.float32)
        for offset in NEIGHBOURS:
            near_index = (slab_index + offset[0]) % NX
            near_off = lax.dynamic_index_in_dim(fluid_offsets, near_index, 1, keepdims=False)
            near_val = lax.dynamic_index_in_dim(field, near_index, 0, keepdims=False)
            near_off = jnp.roll(near_off, (-offset[1], -offset[2]), axis=(1, 2))
            near_val = jnp.roll(near_val, (-offset[1], -offset[2]), axis=(0, 1))
            total = total + pair_kernel(own_off, near_off, offset, near_val)
        return total
    return lax.map(one_slab, jnp.arange(NX, dtype=jnp.int32))


def reference(fluid_offsets, source, marker_offsets, marker_normals, dest_tile, cell_index, grain_velocity, grain_mass):
    cell_count = NX * NY * NZ
    rowsum = weighted(fluid_offsets, jnp.ones(source.shape, jnp.float32))
    diagonal = STIFFEN + rowsum - PER_PARTICLE

    def operate(field):
        return (STIFFEN + rowsum) * field - weighted(fluid_offsets, field)

    fluid_rows = jnp.transpose(fluid_offsets, (1, 2, 3, 0, 4)).reshape(cell_count, 3, 128)
    device_count = N_FLOW * N_CROSS * N_DEPTH
    per_device = G_DEV * MB
    grain_ids = jnp.arange(GRAINS, dtype=jnp.int32)
    depth_of = (grain_ids // G_DEV) % N_DEPTH
    tile_of = dest_tile[:, :, 0]
    flow_of = tile_of // N_CROSS
    cross_of = tile_of % N_CROSS
    local_x = cell_index // (CY * CZ)
    local_y = (cell_index // CZ) % CY
    local_z = cell_index % CZ
    global_x = flow_of * CX + local_x
    global_y = cross_of * CY + local_y
    global_z = depth_of[:, None] * CZ + local_z
    target = ((global_x * NY + global_y) * NZ + global_z).astype(jnp.int32)
    target_groups = target.reshape(device_count, per_device)
    offset_groups = marker_offsets.reshape(device_count, per_device, 3, 128)
    normal_groups = marker_normals.reshape(device_count, per_device, 3, 128)

    velocity = grain_velocity
    displace = jnp.zeros(grain_velocity.shape, jnp.float32)
    pressure = jnp.zeros(source.shape, jnp.float32)
    for step_index in range(STEPS):
        moved = jnp.repeat(displace, MB, axis=0).reshape(device_count, per_device, 3)
        speeds = jnp.repeat(velocity, MB, axis=0).reshape(device_count, per_device, 3)

        def contribute(pieces):
            targets, offsets, normals, shifted, moving = pieces
            positions = offsets + shifted[:, :, None]
            rate = normals[:, 0] * moving[:, 0, None] + normals[:, 1] * moving[:, 1, None] + normals[:, 2] * moving[:, 2, None]
            weight = marker_weights(fluid_rows[targets], positions)
            return jnp.sum(weight * rate[:, None, :], axis=-1)

        added = lax.map(contribute, (target_groups, offset_groups, normal_groups, moved, speeds))
        summed = jnp.zeros((cell_count, 128), jnp.float32).at[target.reshape(-1)].add(added.reshape(-1, 128))
        right_side = source + summed.reshape(source.shape)

        solution = pressure
        residual = right_side - operate(solution)
        precond = residual / diagonal
        direction = precond
        norm_now = jnp.sum(residual * precond)
        for iteration in range(ITERS):
            image = operate(direction)
            alpha = norm_now / jnp.sum(direction * image)
            solution = solution + alpha * direction
            residual = residual - alpha * image
            precond = residual / diagonal
            norm_next = jnp.sum(residual * precond)
            direction = precond + (norm_next / norm_now) * direction
            norm_now = norm_next
        pressure = solution
        pressure_rows = pressure.reshape(cell_count, 128)

        def push(pieces):
            targets, offsets, normals, shifted = pieces
            positions = offsets + shifted[:, :, None]
            weight = marker_weights(fluid_rows[targets], positions)
            felt = jnp.sum(weight * pressure_rows[targets][:, :, None], axis=1)
            return jnp.sum(normals * felt[:, None, :], axis=-1)

        block_force = lax.map(push, (target_groups, offset_groups, normal_groups, moved)).reshape(GRAINS, MB, 3)
        grain_force = jnp.sum(block_force, axis=1)
        velocity = velocity + STEP_TIME * grain_force / grain_mass[:, None]
        displace = displace + STEP_TIME * velocity
    return pressure, velocity
```

```python
import functools

import jax
import jax.numpy as jnp
from jax import lax
from jax.experimental import pallas as pl
from jax.experimental.pallas import tpu as pltpu
from jax.sharding import PartitionSpec as P

STEPS = 2
STIFFEN = 0.5
STEP_TIME = 0.05
PER_PARTICLE = 1.0 / 128.0
ROOT = 1.2011224087864498
SHIFT = (0.0, 0.7, 0.3, 0.5)
CELLS = 16
SLOTS = 512
TILES = 64
CAP = 8
F32 = jnp.float32
BF16 = jnp.bfloat16
VMEM = pltpu.VMEM
SMEM = pltpu.SMEM
NT = (((1,), (1,)), ((), ()))
PAIRS = tuple((i, j) for i in range(4) for j in range(i, 5))


def params(mib):
    return pltpu.CompilerParams(vmem_limit_bytes=mib * 1024 * 1024)


def whole(count, space=VMEM):
    return [pl.BlockSpec(memory_space=space)] * count


def shape(*dims, dtype=F32):
    return jax.ShapeDtypeStruct(dims, dtype)


def inner_pairs():
    out = []
    for c in range(CELLS):
        y, z = c // 4, c % 4
        out.append((c, (0, 0, 0), c))
        if y < 3:
            out.append((c, (0, 1, 0), c + 4))
        if y > 0:
            out.append((c, (0, -1, 0), c - 4))
        if z < 3:
            out.append((c, (0, 0, 1), c + 1))
        if z > 0:
            out.append((c, (0, 0, -1), c - 1))
    return out


def outer_pairs():
    out = []
    for c in range(CELLS):
        y, z = c // 4, c % 4
        out.append((c, (1, 0, 0), (0, c)))
        out.append((c, (-1, 0, 0), (1, c)))
        if y == 3:
            out.append((c, (0, 1, 0), (2, z)))
        if y == 0:
            out.append((c, (0, -1, 0), (3, z)))
        if z == 3:
            out.append((c, (0, 0, 1), (4, y)))
        if z == 0:
            out.append((c, (0, 0, -1), (5, y)))
    return out


INNER = inner_pairs()
OUTER = outer_pairs()


def split2(x):
    high = x.astype(BF16)
    return high, (x - high.astype(F32)).astype(BF16)


def split3(x):
    high = x.astype(BF16)
    rest = x - high.astype(F32)
    middle = rest.astype(BF16)
    return high, middle, (rest - middle.astype(F32)).astype(BF16)


def place_column(total, column, c):
    lane = lax.broadcasted_iota(jnp.int32, (128, 128), 1)
    return jnp.where(lane == c, column, total)


def write_faces(v, faces):
    y0, y3, z0, z3 = faces
    y0[...] = v[0:4, :]
    y3[...] = v[12:16, :]
    for y in range(4):
        z0[y : y + 1, :] = v[4 * y : 4 * y + 1, :]
        z3[y : y + 1, :] = v[4 * y + 3 : 4 * y + 4, :]


def pack_kernel(dest_ref, cell_ref, off_ref, nor_ref, meta_ref, buf_ref, count_ref):
    buf_ref[:, 0:6] = jnp.zeros((TILES, 6, 8, 128), F32)
    meta = meta_ref[...]

    @pl.loop(0, TILES)
    def _(t):
        buf_ref[t, 6] = meta
        count_ref[t] = 0

    lane = lax.broadcasted_iota(jnp.int32, (1, 128), 1)

    @pl.loop(0, 256)
    def _(b):
        d = dest_ref[b]
        r = count_ref[d]
        count_ref[d] = r + 1
        for a in range(3):
            buf_ref[d, a, pl.ds(r, 1), :] = off_ref[b, a : a + 1, :]
            buf_ref[d, 3 + a, pl.ds(r, 1), :] = nor_ref[b, a : a + 1, :]
        code = (cell_ref[b] + 16 * (b // 16)).astype(F32)
        buf_ref[d, 6, 0:1, :] = jnp.where(lane == r, code, buf_ref[d, 6, 0:1, :])


def pack(dest, cell, off, nor, meta):
    return pl.pallas_call(
        pack_kernel,
        out_shape=shape(TILES, 7, 8, 128),
        in_specs=whole(2, SMEM) + whole(3),
        out_specs=pl.BlockSpec(memory_space=VMEM),
        scratch_shapes=[SMEM((TILES,), jnp.int32)],
        compiler_params=params(32),
        name="pack",
    )(dest, cell, off, nor, meta)


def weights_kernel(own_ref, *refs):
    halo, (inner_ref, outer_ref, diag_ref) = refs[:6], refs[6:]
    own = own_ref[...] * ROOT
    columns = jnp.transpose(jnp.concatenate([own, jnp.zeros((80, 128), F32)], axis=0))
    total = jnp.zeros((128, 128), F32)
    inner, outer = list(enumerate(INNER)), list(enumerate(OUTER))
    for c in range(CELLS):
        mine = [columns[:, 16 * a + c : 16 * a + c + 1] for a in range(3)]
        rowsum = jnp.zeros((128, 128), F32)
        for index, (_, step, near) in [p for p in inner if p[1][0] == c]:
            square = None
            for a in range(3):
                gap = (own[16 * a + near : 16 * a + near + 1, :] + step[a] * ROOT) - mine[a]
                square = gap * gap if square is None else square + gap * gap
            weight = jnp.exp2(-square) * PER_PARTICLE
            inner_ref[index] = weight
            rowsum = rowsum + weight
        for index, (_, step, (which, row)) in [p for p in outer if p[1][0] == c]:
            count = 16 if which < 2 else 4
            square = None
            for a in range(3):
                at = count * a + row
                gap = (halo[which][at : at + 1, :] * ROOT + step[a] * ROOT) - mine[a]
                square = gap * gap if square is None else square + gap * gap
            weight = jnp.exp2(-square) * PER_PARTICLE
            outer_ref[index] = weight
            rowsum = rowsum + weight
        total = place_column(total, jnp.sum(rowsum, axis=1, keepdims=True), c)
    diag_ref[...] = jnp.transpose(total)[0:16, :] + (STIFFEN - PER_PARTICLE)


def weights(own, halo):
    return pl.pallas_call(
        weights_kernel,
        out_shape=(shape(len(INNER), 128, 128), shape(len(OUTER), 128, 128), shape(16, 128)),
        in_specs=whole(7),
        out_specs=tuple(whole(3)),
        compiler_params=params(32),
        name="weights",
    )(own, *halo)


def inner_kernel(v_ref, w_ref, out_ref):
    total = jnp.zeros((128, 128), F32)
    for c in range(CELLS):
        product = None
        for index, (cell, _, near) in enumerate(INNER):
            if cell == c:
                term = w_ref[index] * v_ref[near : near + 1, :]
                product = term if product is None else product + term
        total = place_column(total, jnp.sum(product, axis=1, keepdims=True), c)
    out_ref[...] = jnp.transpose(total)[0:16, :]


def apply_inner(v, w):
    return pl.pallas_call(
        inner_kernel,
        out_shape=shape(16, 128),
        in_specs=whole(2),
        out_specs=pl.BlockSpec(memory_space=VMEM),
        compiler_params=params(16),
        cost_estimate=pl.CostEstimate(flops=4 << 20, bytes_accessed=5 << 20, transcendentals=0),
        name="apply_inner",
    )(v, w)


def outer_kernel(k, part_ref, diag_ref, w_ref, *refs):
    halo, basis, outs = refs[:6], refs[6 : 7 + k], refs[7 + k :]
    total = jnp.zeros((128, 128), F32)
    for c in range(CELLS):
        product = None
        for index, (cell, _, (which, row)) in enumerate(OUTER):
            if cell == c:
                term = w_ref[index] * halo[which][row : row + 1, :]
                product = term if product is None else product + term
        total = place_column(total, jnp.sum(product, axis=1, keepdims=True), c)
    image = jnp.transpose(total)[0:16, :] + part_ref[...]
    diag = diag_ref[...]
    v = basis[k][...]
    new = (image - PER_PARTICLE * v) / diag
    if SHIFT[k]:
        new = new - SHIFT[k] * v
    outs[0][...] = new
    if k < 3:
        write_faces(new, outs[1:5])
    else:
        vectors = [ref[...] for ref in basis] + [new]
        rows = []
        for i in range(4):
            scaled = vectors[i] * diag
            for j in range(i, 5):
                rows.append(jnp.sum(scaled * vectors[j], axis=0, keepdims=True))
        rows += [jnp.zeros((1, 128), F32)] * (16 - len(rows))
        outs[1][...] = jnp.concatenate(rows, axis=0)


def apply_outer(k, part, diag, w, halo, basis):
    if k < 3:
        outs = (shape(16, 128),) + (shape(4, 128),) * 4
    else:
        outs = (shape(16, 128), shape(16, 128))
    return pl.pallas_call(
        functools.partial(outer_kernel, k),
        out_shape=outs,
        in_specs=whole(9 + k + 1),
        out_specs=tuple(whole(len(outs))),
        compiler_params=params(16),
        name="apply_outer",
    )(part, diag, w, *halo, *basis)


def coefficients(sums):
    table = {}
    for index, (i, j) in enumerate(PAIRS):
        table[i, j] = table[j, i] = jnp.sum(sums[index : index + 1, :], axis=1, keepdims=True)
    scale, matrix = [], {}
    for i in range(4):
        for j in range(i + 1):
            one = (1.0 - SHIFT[j]) * table[i, j] - table[i, j + 1]
            if i != j:
                two = (1.0 - SHIFT[i]) * table[j, i] - table[j, i + 1]
                one = 0.5 * (one + two)
            matrix[i, j] = one
    for i in range(4):
        scale.append(lax.rsqrt(jnp.maximum(matrix[i, i], 1e-35)))
    right = [table[i, 0] * scale[i] for i in range(4)]
    lower, pivot = {}, []
    for j in range(4):
        value = matrix[j, j] * scale[j] * scale[j]
        for k in range(j):
            value = value - lower[j, k] * lower[j, k] * pivot[k]
        pivot.append(jnp.maximum(value, 3e-7))
        for i in range(j + 1, 4):
            value = matrix[i, j] * scale[i] * scale[j]
            for k in range(j):
                value = value - lower[i, k] * lower[j, k] * pivot[k]
            lower[i, j] = value / pivot[j]
    for i in range(4):
        for k in range(i):
            right[i] = right[i] - lower[i, k] * right[k]
    right = [right[i] / pivot[i] for i in range(4)]
    for i in reversed(range(4)):
        for k in range(i + 1, 4):
            right[i] = right[i] - lower[k, i] * right[k]
    return [right[i] * scale[i] for i in range(4)]


def advance(total, motion, mass, coefs):
    rows = total.shape[0]
    lane = lax.broadcasted_iota(jnp.int32, (rows, 128), 1) % 16
    term = lane % 5
    factor = jnp.ones((rows, 128), F32)
    for k in range(4):
        factor = jnp.where(term == k + 1, coefs[k], factor)
    scaled = jnp.where(lane < 15, total * factor, 0.0)
    force = scaled
    for k in range(1, 5):
        force = force + pltpu.roll(scaled, 128 - k, 1)
    velocity = motion + STEP_TIME * force / mass
    shifted = pltpu.roll(velocity, 1, 1)
    moved = motion + STEP_TIME * shifted
    return jnp.where(lane < 15, jnp.where(term == 0, velocity, jnp.where(term == 1, moved, 0.0)), 0.0)


def marker_kernel(step, *refs):
    if step == 0:
        cells_ref, recv_ref, code_ref, own_ref, source_ref, diag_ref = refs[:6]
        n_ref, added_ref, first_ref, y0, y3, z0, z3 = refs[6:13]
        faces = (y0, y3, z0, z3)
        scratch = refs[13:]
    else:
        cells_ref, recv_ref, code_ref, own_ref, before_ref, diag_ref, payload_ref, motion_ref = refs[:8]
        basis = refs[8:13]
        n_ref, added_ref, first_ref, y0, y3, z0, z3, newmotion_ref, x_ref = refs[13:22]
        faces = (y0, y3, z0, z3)
        scratch = refs[22:]
    table_ref, masked_ref, moving_ref, left_ref = scratch

    if step == 0:
        halves = [recv_ref[:, 6, 1 + h, :] for h in range(2)]
    else:
        coefs = coefficients(payload_ref[128:144, :])
        halves = []
        for h in range(2):
            total = payload_ref[64 * h : 64 * h + 64, :]
            halves.append(advance(total, motion_ref[h], recv_ref[:, 6, 3 + h, :], coefs))
            newmotion_ref[h] = halves[h]

    grain = code_ref[...] // 16
    lane = lax.broadcasted_iota(jnp.int32, (SLOTS, 128), 1) // 16
    for h in range(2):
        for s in range(TILES):
            masked_ref[8 * s : 8 * s + 8, 128 * h : 128 * h + 128] = jnp.broadcast_to(
                halves[h][s : s + 1, :], (8, 128)
            )
        mine = masked_ref[:, 128 * h : 128 * h + 128]
        masked_ref[:, 128 * h : 128 * h + 128] = jnp.where(lane + 8 * h == grain, mine, 0.0)
    where = lax.broadcasted_iota(jnp.int32, (256, 768), 0) % 16
    what = lax.broadcasted_iota(jnp.int32, (256, 768), 1) // 128
    wanted = jnp.where(what < 3, what * 5, (what - 3) * 5 + 1)
    spread = jnp.where(where == wanted, 1.0, 0.0).astype(BF16)
    moving = None
    for piece in split3(masked_ref[...]):
        one = jnp.dot(piece, spread, preferred_element_type=F32)
        moving = one if moving is None else moving + one
    moving_ref[...] = moving

    own = own_ref[...] * ROOT
    columns = jnp.transpose(jnp.concatenate([own, jnp.zeros((80, 128), F32)], axis=0))
    for c in range(CELLS):
        for a in range(3):
            table_ref[c, a] = jnp.broadcast_to(columns[:, 16 * a + c : 16 * a + c + 1], (128, 128))
    added_ref[...] = jnp.zeros((16, 128), F32)

    @pl.loop(0, TILES)
    def _(s):
        rows = pl.ds(pl.multiple_of(s * 8, 8), 8)
        normals = [recv_ref[s, 3 + a] * PER_PARTICLE for a in range(3)]
        place = []
        rate = None
        for a in range(3):
            shift = moving_ref[rows, 384 + 128 * a : 512 + 128 * a]
            place.append((recv_ref[s, a] + shift) * ROOT)
            term = normals[a] * moving_ref[rows, 128 * a : 128 * a + 128]
            rate = term if rate is None else rate + term
        for a, value in enumerate(normals + [rate]):
            high = value.astype(BF16).astype(F32)
            left_ref[:, a, :] = high
            left_ref[:, 4 + a, :] = value - high
        for r in range(8):
            c = cells_ref[s * 8 + r]
            square = None
            for a in range(3):
                gap = table_ref[c, a] - place[a][r : r + 1, :]
                square = gap * gap if square is None else square + gap * gap
            high, low = split2(jnp.exp2(-square))
            left = left_ref[r].astype(BF16)
            both = lax.dot_general(left, high, NT, preferred_element_type=F32)
            both = both + lax.dot_general(left, low, NT, preferred_element_type=F32)
            result = both[0:4, :] + both[4:8, :]
            n_ref[pl.ds(pl.multiple_of(s * 32, 32) + 4 * r, 4), :] = result
            added_ref[pl.ds(c, 1), :] = added_ref[pl.ds(c, 1), :] + result[3:4, :]

    diag = diag_ref[...]
    if step == 0:
        first = (source_ref[...] + added_ref[...]) / diag
    else:
        vectors = [ref[...] for ref in basis]
        x = None
        first = vectors[0] + (added_ref[...] - before_ref[...]) / diag
        for k in range(4):
            term = coefs[k] * vectors[k]
            x = term if x is None else x + term
            first = first - coefs[k] * ((1.0 - SHIFT[k]) * vectors[k] - vectors[k + 1])
        x_ref[...] = x
    first_ref[...] = first
    write_faces(first, faces)


def marker_pass(step, *args):
    outs = (shape(4 * SLOTS, 128), shape(16, 128), shape(16, 128)) + (shape(4, 128),) * 4
    if step:
        outs = outs + (shape(2, TILES, 128), shape(16, 128))
    return pl.pallas_call(
        functools.partial(marker_kernel, step),
        out_shape=outs,
        in_specs=whole(1, SMEM) + whole(len(args) - 1),
        out_specs=tuple(whole(len(outs))),
        scratch_shapes=[
            VMEM((CELLS, 3, 128, 128), F32),
            VMEM((SLOTS, 256), F32),
            VMEM((SLOTS, 768), F32),
            VMEM((8, 8, 128), F32),
        ],
        compiler_params=params(40),
        name="markers",
    )(*args)


def force_kernel(n_ref, code_ref, *refs):
    basis, out_ref = refs[:-1], refs[-1]
    empty = jnp.zeros((16, 128), F32)
    vectors = [ref[...] for ref in basis]
    if len(vectors) == 4:
        vectors = [empty] + vectors
    right_high, right_low = split2(jnp.concatenate(vectors + [empty] * 3, axis=0))
    lane_cell = lax.broadcasted_iota(jnp.int32, (256, 128), 1) % 16
    source = lax.broadcasted_iota(jnp.int32, (128, 256), 0) // 16
    target = lax.broadcasted_iota(jnp.int32, (128, 256), 1) % 16
    spread = jnp.where((target % 5 == source) & (target < 15), 1.0, 0.0).astype(BF16)
    lane = lax.broadcasted_iota(jnp.int32, (256, 256), 1)
    component = lax.broadcasted_iota(jnp.int32, (256, 256), 0) % 4

    @pl.loop(0, 8)
    def _(chunk):
        rows = pl.ds(pl.multiple_of(chunk * 256, 256), 256)
        high, low = split2(n_ref[rows, :])
        dots = lax.dot_general(high, right_high, NT, preferred_element_type=F32)
        dots = dots + lax.dot_general(low, right_high, NT, preferred_element_type=F32)
        dots = dots + lax.dot_general(high, right_low, NT, preferred_element_type=F32)
        code = code_ref[rows, :]
        dots = jnp.where(lane_cell == code % 16, dots, 0.0)
        wide = None
        for piece in split3(dots):
            one = jnp.dot(piece, spread, preferred_element_type=F32)
            wide = one if wide is None else wide + one
        grain = jnp.concatenate([code, code], axis=1) // 16
        keep = (lane // 16 == grain) & ((lane % 16) // 5 == component)
        kept = jnp.sum(jnp.where(keep, wide, 0.0).reshape(8, 32, 256), axis=1)
        out = pl.ds(pl.multiple_of(chunk * 8, 8), 8)
        out_ref[0, out, :] = kept[:, 0:128]
        out_ref[1, out, :] = kept[:, 128:256]


def forces(n, code, basis):
    return pl.pallas_call(
        force_kernel,
        out_shape=shape(2, TILES, 128),
        in_specs=whole(2 + len(basis)),
        out_specs=pl.BlockSpec(memory_space=VMEM),
        compiler_params=params(32),
        cost_estimate=pl.CostEstimate(flops=4 << 20, bytes_accessed=3 << 20, transcendentals=0),
        name="forces",
    )(n, code, *basis)


def final_kernel(payload_ref, motion_ref, mass_ref, x_ref, *refs):
    basis, (out_ref, motion_out_ref) = refs[:4], refs[4:]
    coefs = coefficients(payload_ref[128:144, :])
    x = x_ref[...]
    for k in range(4):
        x = x + coefs[k] * basis[k][...]
    out_ref[...] = x
    for h in range(2):
        total = payload_ref[64 * h : 64 * h + 64, :]
        motion_out_ref[h] = advance(total, motion_ref[h], mass_ref[h], coefs)


def final(payload, motion, mass, x, basis):
    return pl.pallas_call(
        final_kernel,
        out_shape=(shape(16, 128), shape(2, TILES, 128)),
        in_specs=whole(8),
        out_specs=tuple(whole(2)),
        compiler_params=params(16),
        name="final",
    )(payload, motion, mass, x, *basis)


def ring(x, axis, by):
    n = lax.axis_size(axis)
    return lax.ppermute(x, axis, [(i, (i + by) % n) for i in range(n)])


def halo_of(v, y0, y3, z0, z3):
    return (
        ring(v, "flow", -1),
        ring(v, "flow", 1),
        ring(y0, "cross", -1),
        ring(y3, "cross", 1),
        ring(z0, "depth", -1),
        ring(z3, "depth", 1),
    )


def exchange_sum(x, axes):
    for axis in axes:
        n = lax.axis_size(axis)
        m = 1
        while m < n:
            x = x + lax.ppermute(x, axis, [(i, i ^ m) for i in range(n)])
            m *= 2
    return x


def to_lanes(per_grain):
    spread = jnp.pad(per_grain[:, :, None], ((0, 0), (0, 0), (0, 4))).reshape(16, 15)
    return jnp.pad(spread, ((0, 0), (0, 1))).reshape(2, 128)


def per_device(
    fluid_offsets,
    source,
    marker_offsets,
    marker_normals,
    dest_tile,
    cell_index,
    grain_velocity,
    grain_mass,
):
    source = source.reshape(16, 128)
    offs = fluid_offsets.reshape(3, 4, 4, 128)
    own = offs.reshape(48, 128)
    mass_rows = jnp.broadcast_to(grain_mass[:, None], (16, 16)).reshape(2, 128)
    meta = jnp.concatenate(
        [jnp.zeros((1, 128), F32), to_lanes(grain_velocity), mass_rows, jnp.zeros((3, 128), F32)]
    )
    packed = pack(
        dest_tile.reshape(256),
        cell_index.reshape(256),
        marker_offsets.reshape(256, 3, 128),
        marker_normals.reshape(256, 3, 128),
        meta,
    )
    recv = lax.all_to_all(packed, ("flow", "cross"), split_axis=0, concat_axis=0, tiled=True)

    halo = halo_of(
        own,
        offs[:, 0].reshape(12, 128),
        offs[:, 3].reshape(12, 128),
        offs[:, :, 0].reshape(12, 128),
        offs[:, :, 3].reshape(12, 128),
    )
    w_inner, w_outer, diag = weights(own, halo)

    code = recv[:, 6, 0, 0:8].astype(jnp.int32).reshape(SLOTS)
    cells = code % 16
    code_slots = jnp.broadcast_to(code[:, None], (SLOTS, 128))
    code_rows = jnp.broadcast_to(code[:, None, None], (SLOTS, 4, 128)).reshape(4 * SLOTS, 128)
    mass = jnp.stack([recv[:, 6, 3], recv[:, 6, 4]])
    motion = jnp.stack([recv[:, 6, 1], recv[:, 6, 2]])

    x = None
    added = basis = payload = None
    for step in range(STEPS):
        if step == 0:
            n, added, v, *faces = marker_pass(0, cells, recv, code_slots, own, source, diag)
        else:
            n, added, v, *rest = marker_pass(
                1, cells, recv, code_slots, own, added, diag, payload, motion, *basis
            )
            faces, motion, x = rest[:4], rest[4], rest[5]
        basis = [v]
        for k in range(4):
            halo = halo_of(basis[k], *faces)
            part = apply_inner(basis[k], w_inner)
            v, *faces = apply_outer(k, part, diag, w_outer, halo, basis)
            basis.append(v)
        sums = exchange_sum(faces[0], ("depth",))
        felt = forces(n, code_rows, ([x] if step else []) + basis[:4])
        payload = jnp.concatenate([felt.reshape(128, 128), sums])
        payload = exchange_sum(payload, ("flow", "cross"))
    pressure, motion = final(payload, motion, mass, x, basis[:4])
    index = lax.axis_index("flow") * lax.axis_size("cross") + lax.axis_index("cross")
    mine = lax.dynamic_slice_in_dim(motion, index, 1, axis=1).reshape(16, 16)
    velocity = mine[:, 0:15].reshape(16, 3, 5)[:, :, 0]
    return pressure.reshape(1, 4, 4, 128), velocity


def solution(mesh):
    owners = ("flow", "cross", "depth")
    return jax.shard_map(
        per_device,
        mesh=mesh,
        in_specs=(
            P(None, "flow", "cross", "depth", None),
            P("flow", "cross", "depth", None),
            P(owners, None, None, None),
            P(owners, None, None, None),
            P(owners, None, None),
            P(owners, None),
            P(owners, None),
            P(owners),
        ),
        out_specs=(P("flow", "cross", "depth", None), P(owners, None)),
        check_vma=False,
    )
```

```python
import functools

import jax
import jax.numpy as jnp
from jax import lax
from jax.experimental import pallas as pl
from jax.experimental.pallas import tpu as pltpu
from jax.sharding import PartitionSpec as P

STEPS = 2
STIFFEN = 0.5
STEP_TIME = 0.05
PER_PARTICLE = 1.0 / 128.0
ROOT = 1.2011224087864498
SHIFT = (0.0, 0.7, 0.3, 0.5)
CELLS = 16
SLOTS = 512
TILES = 64
CAP = 8
F32 = jnp.float32
BF16 = jnp.bfloat16
VMEM = pltpu.VMEM
SMEM = pltpu.SMEM
NT = (((1,), (1,)), ((), ()))
PAIRS = tuple((i, j) for i in range(4) for j in range(i, 5))


def params(mib):
    return pltpu.CompilerParams(vmem_limit_bytes=mib * 1024 * 1024)


def whole(count, space=VMEM):
    return [pl.BlockSpec(memory_space=space)] * count


def shape(*dims, dtype=F32):
    return jax.ShapeDtypeStruct(dims, dtype)


def inner_pairs():
    out = []
    for c in range(CELLS):
        y, z = c // 4, c % 4
        out.append((c, (0, 0, 0), c))
        if y < 3:
            out.append((c, (0, 1, 0), c + 4))
        if y > 0:
            out.append((c, (0, -1, 0), c - 4))
        if z < 3:
            out.append((c, (0, 0, 1), c + 1))
        if z > 0:
            out.append((c, (0, 0, -1), c - 1))
    return out


def outer_pairs():
    out = []
    for c in range(CELLS):
        y, z = c // 4, c % 4
        out.append((c, (1, 0, 0), (0, c)))
        out.append((c, (-1, 0, 0), (1, c)))
        if y == 3:
            out.append((c, (0, 1, 0), (2, z)))
        if y == 0:
            out.append((c, (0, -1, 0), (3, z)))
        if z == 3:
            out.append((c, (0, 0, 1), (4, y)))
        if z == 0:
            out.append((c, (0, 0, -1), (5, y)))
    return out


INNER = inner_pairs()
OUTER = outer_pairs()


def split2(x):
    high = x.astype(BF16)
    return high, (x - high.astype(F32)).astype(BF16)


def split3(x):
    high = x.astype(BF16)
    rest = x - high.astype(F32)
    middle = rest.astype(BF16)
    return high, middle, (rest - middle.astype(F32)).astype(BF16)


def place_column(total, column, c):
    lane = lax.broadcasted_iota(jnp.int32, (128, 128), 1)
    return jnp.where(lane == c, column, total)


def write_faces(v, faces):
    y0, y3, z0, z3 = faces
    y0[...] = v[0:4, :]
    y3[...] = v[12:16, :]
    for y in range(4):
        z0[y : y + 1, :] = v[4 * y : 4 * y + 1, :]
        z3[y : y + 1, :] = v[4 * y + 3 : 4 * y + 4, :]


def pack_kernel(dest_ref, cell_ref, off_ref, nor_ref, meta_ref, buf_ref, count_ref):
    buf_ref[:, 0:48, :] = jnp.zeros((TILES, 48, 128), F32)
    meta = meta_ref[...]

    @pl.loop(0, TILES)
    def _(t):
        buf_ref[t, 48:56, :] = meta
        count_ref[t] = 0

    lane = lax.broadcasted_iota(jnp.int32, (1, 128), 1)

    @pl.loop(0, 16)
    def _(g):
        off = [(off_ref[g, a] - 0.5) * ROOT for a in range(3)]
        nor = [nor_ref[g, a] * PER_PARTICLE for a in range(3)]
        for b in range(16):
            d = dest_ref[g, b]
            r = count_ref[d]
            count_ref[d] = r + 1
            for a in range(3):
                buf_ref[d, pl.ds(6 * r + a, 1), :] = off[a][b : b + 1, :]
                buf_ref[d, pl.ds(6 * r + 3 + a, 1), :] = nor[a][b : b + 1, :]
            code = (cell_ref[g, b] + 16 * g).astype(F32)
            buf_ref[d, 48:49, :] = jnp.where(lane == r, code, buf_ref[d, 48:49, :])


def pack(dest, cell, off, nor, meta):
    return pl.pallas_call(
        pack_kernel,
        out_shape=shape(TILES, 56, 128),
        in_specs=whole(2, SMEM) + whole(3),
        out_specs=pl.BlockSpec(memory_space=VMEM),
        scratch_shapes=[SMEM((TILES,), jnp.int32)],
        compiler_params=params(32),
        cost_estimate=pl.CostEstimate(flops=4 << 20, bytes_accessed=16 << 20, transcendentals=0),
        name="pack",
    )(dest, cell, off, nor, meta)


def weights_kernel(own_ref, *refs):
    halo, (inner_ref, outer_ref, diag_ref) = refs[:6], refs[6:]
    own = own_ref[...] * ROOT
    columns = jnp.transpose(jnp.concatenate([own, jnp.zeros((80, 128), F32)], axis=0))
    total = jnp.zeros((128, 128), F32)
    inner, outer = list(enumerate(INNER)), list(enumerate(OUTER))
    for c in range(CELLS):
        mine = [columns[:, 16 * a + c : 16 * a + c + 1] for a in range(3)]
        rowsum = jnp.zeros((128, 128), F32)
        for index, (_, step, near) in [p for p in inner if p[1][0] == c]:
            square = None
            for a in range(3):
                gap = (own[16 * a + near : 16 * a + near + 1, :] + step[a] * ROOT) - mine[a]
                square = gap * gap if square is None else square + gap * gap
            weight = jnp.exp2(-square) * PER_PARTICLE
            inner_ref[index] = weight
            rowsum = rowsum + weight
        for index, (_, step, (which, row)) in [p for p in outer if p[1][0] == c]:
            count = 16 if which < 2 else 4
            square = None
            for a in range(3):
                at = count * a + row
                gap = (halo[which][at : at + 1, :] * ROOT + step[a] * ROOT) - mine[a]
                square = gap * gap if square is None else square + gap * gap
            weight = jnp.exp2(-square) * PER_PARTICLE
            outer_ref[index] = weight
            rowsum = rowsum + weight
        total = place_column(total, jnp.sum(rowsum, axis=1, keepdims=True), c)
    diag_ref[...] = jnp.transpose(total)[0:16, :] + (STIFFEN - PER_PARTICLE)


def weights(own, halo):
    return pl.pallas_call(
        weights_kernel,
        out_shape=(shape(len(INNER), 128, 128), shape(len(OUTER), 128, 128), shape(16, 128)),
        in_specs=whole(7),
        out_specs=tuple(whole(3)),
        compiler_params=params(32),
        name="weights",
    )(own, *halo)


def inner_kernel(v_ref, w_ref, out_ref):
    total = jnp.zeros((128, 128), F32)
    for c in range(CELLS):
        product = None
        for index, (cell, _, near) in enumerate(INNER):
            if cell == c:
                term = w_ref[index] * v_ref[near : near + 1, :]
                product = term if product is None else product + term
        total = place_column(total, jnp.sum(product, axis=1, keepdims=True), c)
    out_ref[...] = jnp.transpose(total)[0:16, :]


def apply_inner(v, w):
    return pl.pallas_call(
        inner_kernel,
        out_shape=shape(16, 128),
        in_specs=whole(2),
        out_specs=pl.BlockSpec(memory_space=VMEM),
        compiler_params=params(16),
        cost_estimate=pl.CostEstimate(flops=4 << 20, bytes_accessed=5 << 20, transcendentals=0),
        name="apply_inner",
    )(v, w)


def outer_kernel(k, part_ref, diag_ref, w_ref, *refs):
    halo, basis, outs = refs[:6], refs[6 : 7 + k], refs[7 + k :]
    total = jnp.zeros((128, 128), F32)
    for c in range(CELLS):
        product = None
        for index, (cell, _, (which, row)) in enumerate(OUTER):
            if cell == c:
                term = w_ref[index] * halo[which][row : row + 1, :]
                product = term if product is None else product + term
        total = place_column(total, jnp.sum(product, axis=1, keepdims=True), c)
    image = jnp.transpose(total)[0:16, :] + part_ref[...]
    diag = diag_ref[...]
    v = basis[k][...]
    new = (image - PER_PARTICLE * v) / diag
    if SHIFT[k]:
        new = new - SHIFT[k] * v
    outs[0][...] = new
    if k < 3:
        write_faces(new, outs[1:5])
    else:
        vectors = [ref[...] for ref in basis] + [new]
        rows = []
        for i in range(4):
            scaled = vectors[i] * diag
            for j in range(i, 5):
                rows.append(jnp.sum(scaled * vectors[j], axis=0, keepdims=True))
        rows.append(jnp.zeros((128 - len(rows), 128), F32))
        lanes = jnp.sum(jnp.transpose(jnp.concatenate(rows, axis=0)), axis=0, keepdims=True)
        outs[1][...] = jnp.broadcast_to(lanes, (8, 128))


def apply_outer(k, part, diag, w, halo, basis):
    if k < 3:
        outs = (shape(16, 128),) + (shape(4, 128),) * 4
    else:
        outs = (shape(16, 128), shape(8, 128))
    return pl.pallas_call(
        functools.partial(outer_kernel, k),
        out_shape=outs,
        in_specs=whole(9 + k + 1),
        out_specs=tuple(whole(len(outs))),
        compiler_params=params(16),
        name="apply_outer",
    )(part, diag, w, *halo, *basis)


def coefficients(sums):
    table = {}
    lane = lax.broadcasted_iota(jnp.int32, (1, 128), 1)
    for index, (i, j) in enumerate(PAIRS):
        one = jnp.sum(jnp.where(lane == index, sums, 0.0), axis=1, keepdims=True)
        table[i, j] = table[j, i] = one
    scale, matrix = [], {}
    for i in range(4):
        for j in range(i + 1):
            one = (1.0 - SHIFT[j]) * table[i, j] - table[i, j + 1]
            if i != j:
                two = (1.0 - SHIFT[i]) * table[j, i] - table[j, i + 1]
                one = 0.5 * (one + two)
            matrix[i, j] = one
    for i in range(4):
        scale.append(lax.rsqrt(jnp.maximum(matrix[i, i], 1e-35)))
    right = [table[i, 0] * scale[i] for i in range(4)]
    lower, pivot = {}, []
    for j in range(4):
        value = matrix[j, j] * scale[j] * scale[j]
        for k in range(j):
            value = value - lower[j, k] * lower[j, k] * pivot[k]
        pivot.append(jnp.maximum(value, 3e-7))
        for i in range(j + 1, 4):
            value = matrix[i, j] * scale[i] * scale[j]
            for k in range(j):
                value = value - lower[i, k] * lower[j, k] * pivot[k]
            lower[i, j] = value / pivot[j]
    for i in range(4):
        for k in range(i):
            right[i] = right[i] - lower[i, k] * right[k]
    right = [right[i] / pivot[i] for i in range(4)]
    for i in reversed(range(4)):
        for k in range(i + 1, 4):
            right[i] = right[i] - lower[k, i] * right[k]
    return [right[i] * scale[i] for i in range(4)]


def advance(total, motion, mass, coefs, lanes):
    lane = lax.broadcasted_iota(jnp.int32, total.shape, 1)
    term = (lane >> 4) & 3
    factor = jnp.zeros(total.shape, F32)
    for k in range(4):
        factor = jnp.where(term == k, coefs[k], factor)
    scaled = jnp.where(lane < lanes, total * factor, 0.0)
    force = scaled
    for k in range(1, 4):
        force = force + pltpu.roll(scaled, 128 - 16 * k, 1)
    velocity = motion + STEP_TIME * force / mass
    moved = motion + STEP_TIME * pltpu.roll(velocity, 16, 1)
    kept = jnp.where(term == 0, velocity, jnp.where(term == 1, moved, 0.0))
    return jnp.where(lane < lanes, kept, 0.0)


def marker_kernel(step, *refs):
    if step == 0:
        codes_ref, recv_ref, feature_ref, source_ref, diag_ref = refs[:5]
        n_ref, added_ref, first_ref, y0, y3, z0, z3, rows_ref, moving_ref = refs[5:14]
        scratch = refs[14:]
    else:
        codes_ref, recv_ref, feature_ref, before_ref, diag_ref, payload_ref, motion_ref = refs[:7]
        basis = refs[7:12]
        n_ref, added_ref, first_ref, y0, y3, z0, z3, x_ref, moving_ref = refs[12:21]
        scratch = refs[21:]
    tile_ref, total_ref, even_ref, odd_ref = scratch

    if step == 0:
        moving_ref[0] = recv_ref[:, 49, :]
        moving_ref[1] = recv_ref[:, 50, :]
    else:
        coefs = coefficients(payload_ref[96:97, :])
        mass = recv_ref[:, 51, :]
        part = payload_ref[64:96, :]
        second = jnp.concatenate([part, pltpu.roll(part, 64, 1)], axis=0)
        moving_ref[0] = advance(payload_ref[0:64, :], motion_ref[0], mass, coefs, 128)
        moving_ref[1] = advance(second, motion_ref[1], mass, coefs, 64)

    row = lax.broadcasted_iota(jnp.int32, (8, 128), 0)
    lane = lax.broadcasted_iota(jnp.int32, (8, 128), 1)
    pick = jnp.where(row < 3, row * 4 + 1, jnp.where(row < 6, (row - 3) * 4, 32)) * 16
    scale = jnp.where(row < 3, ROOT, 1.0)

    @pl.loop(0, TILES)
    def _(s):
        low = jnp.broadcast_to(moving_ref[0, pl.ds(s, 1), :], (8, 128))
        high = jnp.broadcast_to(moving_ref[1, pl.ds(s, 1), :], (8, 128))
        for r in range(8):
            target = pick + (codes_ref[s * 8 + r] >> 4)
            chosen = jnp.where(lane == target, low, jnp.where(lane + 128 == target, high, 0.0))
            tile_ref[s, r] = jnp.broadcast_to(jnp.sum(chosen, axis=1, keepdims=True), (8, 128)) * scale

    total_ref[...] = jnp.zeros((CELLS, 8, 128), F32)

    def weigh(s, r, buffer_ref):
        c = codes_ref[s * 8 + r] & 15
        place = recv_ref[s, 6 * r : 6 * r + 8, :] + tile_ref[s, r]
        high = place.astype(BF16).astype(F32)
        square = jnp.sum(jnp.where(row < 3, place * place, 0.0), axis=0, keepdims=True)
        square = jnp.broadcast_to(square, (8, 128))
        first = square.astype(BF16).astype(F32)
        second = (square - first).astype(BF16).astype(F32)
        third = square - first - second
        ends = jnp.where(row == 0, first, jnp.where(row == 1, second, jnp.where(row == 2, third, 1.0)))
        right = jnp.concatenate([high, place - high, high, ends], axis=0).astype(BF16)
        power = jnp.dot(feature_ref[c], right, preferred_element_type=F32)
        upper, lower = split2(jnp.exp2(power))
        buffer_ref[r, 0:128, :] = upper
        buffer_ref[r, 128:256, :] = lower

    def contract(s, r, buffer_ref):
        left = jnp.concatenate(split2(recv_ref[s, 6 * r : 6 * r + 8, :]), axis=0)
        both = lax.dot_general(left, buffer_ref[r], NT, preferred_element_type=F32)
        return both[0:8, 0:128] + both[8:16, 0:128] + both[0:8, 128:256]

    def turn(s_next, next_ref, s_now, now_ref):
        results = []
        for r in range(8):
            weigh(s_next, r, next_ref)
            results.append(contract(s_now, r, now_ref))
        for r in range(8):
            c = codes_ref[s_now * 8 + r] & 15
            total_ref[c] = total_ref[c] + results[r] * tile_ref[s_now, r]
            if r % 2 == 1:
                pair = pl.ds(pl.multiple_of(s_now * 32, 32) + 4 * (r - 1), 8)
                below, above = pltpu.roll(results[r - 1], 5, 0), pltpu.roll(results[r], 1, 0)
                n_ref[pair, :] = jnp.where(row < 4, below, above)
                if step == 0:
                    rows_ref[pair, :] = jnp.where(
                        row < 4, codes_ref[s_now * 8 + r - 1], codes_ref[s_now * 8 + r]
                    )

    for r in range(8):
        weigh(0, r, even_ref)

    @pl.loop(0, TILES // 2)
    def _(t):
        turn(2 * t + 1, odd_ref, 2 * t, even_ref)
        turn(jnp.minimum(2 * t + 2, TILES - 1), even_ref, 2 * t + 1, odd_ref)

    for c in range(CELLS):
        added_ref[c : c + 1, :] = jnp.sum(total_ref[c][3:6, :], axis=0, keepdims=True)
    diag = diag_ref[...]
    if step == 0:
        first = (source_ref[...] + added_ref[...]) / diag
    else:
        vectors = [ref[...] for ref in basis]
        x = None
        first = vectors[0] + (added_ref[...] - before_ref[...]) / diag
        for k in range(4):
            term = coefs[k] * vectors[k]
            x = term if x is None else x + term
            first = first - coefs[k] * ((1.0 - SHIFT[k]) * vectors[k] - vectors[k + 1])
        x_ref[...] = x
    first_ref[...] = first
    write_faces(first, (y0, y3, z0, z3))


def marker_pass(step, *args):
    outs = (shape(4 * SLOTS, 128), shape(16, 128), shape(16, 128)) + (shape(4, 128),) * 4
    outs = outs + (shape(16, 128) if step else shape(4 * SLOTS, 128, dtype=jnp.int32),)
    outs = outs + (shape(2, TILES, 128),)
    return pl.pallas_call(
        functools.partial(marker_kernel, step),
        out_shape=outs,
        in_specs=whole(1, SMEM) + whole(len(args) - 1),
        out_specs=tuple(whole(len(outs))),
        scratch_shapes=[
            VMEM((TILES, 8, 8, 128), F32),
            VMEM((CELLS, 8, 128), F32),
            VMEM((8, 256, 128), BF16),
            VMEM((8, 256, 128), BF16),
        ],
        compiler_params=params(32),
        name="markers",
    )(*args)


def features(own):
    def rounded(x):
        return lax.reduce_precision(x, 8, 7)

    o = (own.reshape(3, CELLS, 128) - 0.5) * ROOT
    high = rounded(2.0 * o)
    middle = rounded(2.0 * o - high)
    square = o[0] * o[0] + o[1] * o[1] + o[2] * o[2]
    first = rounded(square)
    second = rounded(square - first)
    third = square - first - second
    five, two = jnp.zeros((5, CELLS, 128), F32), jnp.zeros((2, CELLS, 128), F32)
    ends = jnp.concatenate([-jnp.ones((3, CELLS, 128), F32), -jnp.stack([first, second, third]), two])
    rows = jnp.concatenate([high, five, high, five, middle, five, ends])
    return jnp.transpose(rows, (1, 2, 0)).astype(BF16)


def force_kernel(n_ref, rows_ref, *refs):
    basis, out_ref, wide_ref = refs[:-2], refs[-2], refs[-1]
    count = len(basis)
    empty = jnp.zeros((16, 128), F32)
    vectors = [ref[...] for ref in basis]
    right_high, right_low = split2(jnp.concatenate(vectors + [empty] * (8 - count), axis=0))
    lane_cell = lax.broadcasted_iota(jnp.int32, (256, 128), 1) & 15
    source = lax.broadcasted_iota(jnp.int32, (128, 256), 0) >> 4
    target = lax.broadcasted_iota(jnp.int32, (128, 256), 1) >> 4
    spread = jnp.where((target % count == source) & (target < 3 * count), 1.0, 0.0).astype(BF16)
    lane = lax.broadcasted_iota(jnp.int32, (256, 256), 1)
    component = lax.broadcasted_iota(jnp.int32, (256, 256), 0) & 3
    fits = (lane >> 4) // count == component
    lane_grain = jnp.where(fits, lane & 15, -1)

    @pl.loop(0, 8)
    def _(chunk):
        rows = pl.ds(pl.multiple_of(chunk * 256, 256), 256)
        high, low = split2(n_ref[rows, :])
        dots = lax.dot_general(high, right_high, NT, preferred_element_type=F32)
        dots = dots + lax.dot_general(low, right_high, NT, preferred_element_type=F32)
        dots = dots + lax.dot_general(high, right_low, NT, preferred_element_type=F32)
        code = rows_ref[rows, :]
        dots = jnp.where(lane_cell == (code & 15), dots, 0.0)
        wide = None
        for piece in split3(dots):
            one = jnp.dot(piece, spread, preferred_element_type=F32)
            wide = one if wide is None else wide + one
        grain = jnp.concatenate([code, code], axis=1) >> 4
        kept = jnp.where(lane_grain == grain, wide, 0.0).reshape(8, 32, 256)
        wide_ref[pl.ds(pl.multiple_of(chunk * 8, 8), 8), :] = jnp.sum(kept, axis=1)

    if count == 4:
        out_ref[0:64, :] = wide_ref[:, 0:128]
        half = lax.broadcasted_iota(jnp.int32, (32, 128), 1) < 64
        below = pltpu.roll(wide_ref[32:64, 128:256], 64, 1)
        out_ref[64:96, :] = jnp.where(half, wide_ref[0:32, 128:256], below)
    else:
        out_ref[...] = wide_ref[...]


def forces(n, rows, basis):
    return pl.pallas_call(
        force_kernel,
        out_shape=shape(96, 128) if len(basis) == 4 else shape(64, 256),
        in_specs=whole(2 + len(basis)),
        out_specs=pl.BlockSpec(memory_space=VMEM),
        scratch_shapes=[VMEM((64, 256), F32)],
        compiler_params=params(32),
        cost_estimate=pl.CostEstimate(flops=4 << 20, bytes_accessed=16 << 20, transcendentals=0),
        name="forces",
    )(n, rows, *basis)


def final_kernel(got_ref, x_ref, *refs):
    basis, (out_ref, scaled_ref) = refs[:4], refs[4:]
    got = [jnp.sum(got_ref[:, h, :], axis=0, keepdims=True) for h in range(3)]
    coefs = coefficients(got[2])
    x = x_ref[...]
    for k in range(4):
        x = x + coefs[k] * basis[k][...]
    out_ref[...] = x
    for h in range(2):
        term = (lax.broadcasted_iota(jnp.int32, (1, 128), 1) // 16 + 8 * h) % 5
        factor = jnp.ones((1, 128), F32)
        for k in range(4):
            factor = jnp.where(term == k + 1, coefs[k], factor)
        scaled_ref[h : h + 1, :] = got[h] * factor


def final(got, x, basis):
    return pl.pallas_call(
        final_kernel,
        out_shape=(shape(16, 128), shape(2, 128)),
        in_specs=whole(6),
        out_specs=tuple(whole(2)),
        compiler_params=params(16),
        name="final",
    )(got, x, *basis)


def ring(x, axis, by):
    n = lax.axis_size(axis)
    return lax.ppermute(x, axis, [(i, (i + by) % n) for i in range(n)])


def halo_of(v, y0, y3, z0, z3):
    return (
        ring(v, "flow", -1),
        ring(v, "flow", 1),
        ring(y0, "cross", -1),
        ring(y3, "cross", 1),
        ring(z0, "depth", -1),
        ring(z3, "depth", 1),
    )


def exchange_sum(x, axes):
    for axis in axes:
        n = lax.axis_size(axis)
        m = 1
        while m < n:
            x = x + lax.ppermute(x, axis, [(i, i ^ m) for i in range(n)])
            m *= 2
    return x


def per_device(
    fluid_offsets,
    source,
    marker_offsets,
    marker_normals,
    dest_tile,
    cell_index,
    grain_velocity,
    grain_mass,
):
    source = source.reshape(16, 128)
    offs = fluid_offsets.reshape(3, 4, 4, 128)
    own = offs.reshape(48, 128)
    lanes = jnp.pad(jnp.transpose(grain_velocity), ((0, 1), (0, 48))).reshape(2, 128)
    mass = jnp.broadcast_to(grain_mass[None, :], (8, 16)).reshape(1, 128)
    meta = jnp.concatenate([jnp.zeros((1, 128), F32), lanes, mass, jnp.zeros((4, 128), F32)])
    halo = halo_of(
        own,
        offs[:, 0].reshape(12, 128),
        offs[:, 3].reshape(12, 128),
        offs[:, :, 0].reshape(12, 128),
        offs[:, :, 3].reshape(12, 128),
    )
    packed = pack(
        dest_tile.reshape(16, 16),
        cell_index,
        jnp.transpose(marker_offsets, (0, 2, 1, 3)),
        jnp.transpose(marker_normals, (0, 2, 1, 3)),
        meta,
    )
    packed, halo = lax.optimization_barrier((packed, halo))
    recv = lax.all_to_all(packed, ("flow", "cross"), split_axis=0, concat_axis=0, tiled=True)
    w_inner, w_outer, diag = weights(own, halo)
    feature = features(own)
    codes = recv[:, 48, 0:8].astype(jnp.int32).reshape(SLOTS)

    x = None
    n = rows = motion = added = basis = payload = None
    for step in range(STEPS):
        if step == 0:
            n, added, v, *rest = marker_pass(0, codes, recv, feature, source, diag)
            faces, rows, motion = rest[:4], rest[4], rest[5]
        else:
            n, added, v, *rest = marker_pass(
                1, codes, recv, feature, added, diag, payload, motion, *basis
            )
            faces, x, motion = rest[:4], rest[4], rest[5]
        basis = [v]
        for k in range(4):
            halo = halo_of(basis[k], *faces)
            part = apply_inner(basis[k], w_inner)
            v, *faces = apply_outer(k, part, diag, w_outer, halo, basis)
            basis.append(v)
        sums = exchange_sum(faces[0], ("depth",))
        if step < STEPS - 1:
            felt = forces(n, rows, basis[:4])
            payload = exchange_sum(jnp.concatenate([felt, sums]), ("flow", "cross"))
    felt = forces(n, rows, [x] + basis[:4]).reshape(TILES, 2, 128)
    send = jnp.concatenate([felt, jnp.broadcast_to(sums[0:1], (TILES, 1, 128))], axis=1)
    got = lax.all_to_all(send, ("flow", "cross"), split_axis=0, concat_axis=0, tiled=True)
    pressure, scaled = final(got, x, basis[:4])
    force = jnp.sum(scaled.reshape(256)[:240].reshape(3, 5, 16), axis=1)
    index = lax.axis_index("flow") * lax.axis_size("cross") + lax.axis_index("cross")
    mine = lax.dynamic_slice_in_dim(motion, index, 1, axis=1).reshape(4, 64)[:3, :16]
    velocity = jnp.transpose(mine + STEP_TIME * force / grain_mass[None, :])
    return pressure.reshape(1, 4, 4, 128), velocity


def solution(mesh):
    owners = ("flow", "cross", "depth")
    return jax.shard_map(
        per_device,
        mesh=mesh,
        in_specs=(
            P(None, "flow", "cross", "depth", None),
            P("flow", "cross", "depth", None),
            P(owners, None, None, None),
            P(owners, None, None, None),
            P(owners, None, None),
            P(owners, None),
            P(owners, None),
            P(owners),
        ),
        out_specs=(P("flow", "cross", "depth", None), P(owners, None)),
        check_vma=False,
    )
```

```python
import functools

import jax
import jax.numpy as jnp
from jax import lax
from jax.experimental import pallas as pl
from jax.experimental.pallas import tpu as pltpu
from jax.sharding import PartitionSpec as P

STEPS = 2
STIFFEN = 0.5
STEP_TIME = 0.05
PER_PARTICLE = 1.0 / 128.0
ROOT = 1.2011224087864498
SHIFT = (0.0, 0.7, 0.3, 0.5)
CELLS = 16
SLOTS = 512
TILES = 64
CAP = 8
F32 = jnp.float32
BF16 = jnp.bfloat16
VMEM = pltpu.VMEM
SMEM = pltpu.SMEM
NT = (((1,), (1,)), ((), ()))
PAIRS = tuple((i, j) for i in range(4) for j in range(i, 5))


def params(mib):
    return pltpu.CompilerParams(vmem_limit_bytes=mib * 1024 * 1024)


def whole(count, space=VMEM):
    return [pl.BlockSpec(memory_space=space)] * count


def shape(*dims, dtype=F32):
    return jax.ShapeDtypeStruct(dims, dtype)


def inner_pairs():
    out = []
    for c in range(CELLS):
        y, z = c // 4, c % 4
        out.append((c, (0, 0, 0), c))
        if y < 3:
            out.append((c, (0, 1, 0), c + 4))
        if y > 0:
            out.append((c, (0, -1, 0), c - 4))
        if z < 3:
            out.append((c, (0, 0, 1), c + 1))
        if z > 0:
            out.append((c, (0, 0, -1), c - 1))
    return out


def outer_pairs():
    out = []
    for c in range(CELLS):
        y, z = c // 4, c % 4
        out.append((c, (1, 0, 0), (0, c)))
        out.append((c, (-1, 0, 0), (1, c)))
        if y == 3:
            out.append((c, (0, 1, 0), (2, z)))
        if y == 0:
            out.append((c, (0, -1, 0), (3, z)))
        if z == 3:
            out.append((c, (0, 0, 1), (4, y)))
        if z == 0:
            out.append((c, (0, 0, -1), (5, y)))
    return out


INNER = inner_pairs()
OUTER = outer_pairs()


def split2(x):
    high = x.astype(BF16)
    return high, (x - high.astype(F32)).astype(BF16)


def split3(x):
    high = x.astype(BF16)
    rest = x - high.astype(F32)
    middle = rest.astype(BF16)
    return high, middle, (rest - middle.astype(F32)).astype(BF16)


def place_column(total, column, c):
    lane = lax.broadcasted_iota(jnp.int32, (128, 128), 1)
    return jnp.where(lane == c, column, total)


def write_faces(v, faces):
    y0, y3, z0, z3 = faces
    y0[...] = v[0:4, :]
    y3[...] = v[12:16, :]
    for y in range(4):
        z0[y : y + 1, :] = v[4 * y : 4 * y + 1, :]
        z3[y : y + 1, :] = v[4 * y + 3 : 4 * y + 4, :]


def pack_kernel(dest_ref, cell_ref, off_ref, nor_ref, meta_ref, buf_ref, count_ref):
    buf_ref[:, 0:48, :] = jnp.zeros((TILES, 48, 128), F32)
    meta = meta_ref[...]

    @pl.loop(0, TILES)
    def _(t):
        buf_ref[t, 48:56, :] = meta
        count_ref[t] = 0

    lane = lax.broadcasted_iota(jnp.int32, (1, 128), 1)

    @pl.loop(0, 16)
    def _(g):
        off = [(off_ref[g, a] - 0.5) * ROOT for a in range(3)]
        nor = [nor_ref[g, a] * PER_PARTICLE for a in range(3)]
        for b in range(16):
            d = dest_ref[g, b]
            r = count_ref[d]
            count_ref[d] = r + 1
            for a in range(3):
                buf_ref[d, pl.ds(6 * r + a, 1), :] = off[a][b : b + 1, :]
                buf_ref[d, pl.ds(6 * r + 3 + a, 1), :] = nor[a][b : b + 1, :]
            code = (cell_ref[g, b] + 16 * g).astype(F32)
            buf_ref[d, 48:49, :] = jnp.where(lane == r, code, buf_ref[d, 48:49, :])


def pack(dest, cell, off, nor, meta):
    return pl.pallas_call(
        pack_kernel,
        out_shape=shape(TILES, 56, 128),
        in_specs=whole(2, SMEM) + whole(3),
        out_specs=pl.BlockSpec(memory_space=VMEM),
        scratch_shapes=[SMEM((TILES,), jnp.int32)],
        compiler_params=params(32),
        cost_estimate=pl.CostEstimate(flops=4 << 20, bytes_accessed=16 << 20, transcendentals=0),
        name="pack",
    )(dest, cell, off, nor, meta)


def weights_kernel(own_ref, source_ref, added_ref, *refs):
    halo, (inner_ref, outer_ref, diag_ref, first_ref, *faces) = refs[:6], refs[6:]
    own = own_ref[...] * ROOT
    columns = jnp.transpose(jnp.concatenate([own, jnp.zeros((80, 128), F32)], axis=0))
    total = jnp.zeros((128, 128), F32)
    inner, outer = list(enumerate(INNER)), list(enumerate(OUTER))
    for c in range(CELLS):
        mine = [columns[:, 16 * a + c : 16 * a + c + 1] for a in range(3)]
        rowsum = jnp.zeros((128, 128), F32)
        for index, (_, step, near) in [p for p in inner if p[1][0] == c]:
            square = None
            for a in range(3):
                gap = (own[16 * a + near : 16 * a + near + 1, :] + step[a] * ROOT) - mine[a]
                square = gap * gap if square is None else square + gap * gap
            weight = jnp.exp2(-square) * PER_PARTICLE
            inner_ref[index] = weight
            rowsum = rowsum + weight
        for index, (_, step, (which, row)) in [p for p in outer if p[1][0] == c]:
            count = 16 if which < 2 else 4
            square = None
            for a in range(3):
                at = count * a + row
                gap = (halo[which][at : at + 1, :] * ROOT + step[a] * ROOT) - mine[a]
                square = gap * gap if square is None else square + gap * gap
            weight = jnp.exp2(-square) * PER_PARTICLE
            outer_ref[index] = weight
            rowsum = rowsum + weight
        total = place_column(total, jnp.sum(rowsum, axis=1, keepdims=True), c)
    diag = jnp.transpose(total)[0:16, :] + (STIFFEN - PER_PARTICLE)
    diag_ref[...] = diag
    first = (source_ref[...] + added_ref[...]) / diag
    first_ref[...] = first
    write_faces(first, faces)


def weights(own, source, added, halo):
    outs = (shape(len(INNER), 128, 128), shape(len(OUTER), 128, 128), shape(16, 128), shape(16, 128))
    return pl.pallas_call(
        weights_kernel,
        out_shape=outs + (shape(4, 128),) * 4,
        in_specs=whole(9),
        out_specs=tuple(whole(8)),
        compiler_params=params(32),
        name="weights",
    )(own, source, added, *halo)


def inner_kernel(v_ref, w_ref, out_ref):
    total = jnp.zeros((128, 128), F32)
    for c in range(CELLS):
        product = None
        for index, (cell, _, near) in enumerate(INNER):
            if cell == c:
                term = w_ref[index] * v_ref[near : near + 1, :]
                product = term if product is None else product + term
        total = place_column(total, jnp.sum(product, axis=1, keepdims=True), c)
    out_ref[...] = jnp.transpose(total)[0:16, :]


def apply_inner(v, w):
    return pl.pallas_call(
        inner_kernel,
        out_shape=shape(16, 128),
        in_specs=whole(2),
        out_specs=pl.BlockSpec(memory_space=VMEM),
        compiler_params=params(16),
        cost_estimate=pl.CostEstimate(flops=4 << 20, bytes_accessed=5 << 20, transcendentals=0),
        name="apply_inner",
    )(v, w)


def outer_kernel(k, part_ref, diag_ref, w_ref, *refs):
    halo, basis, outs = refs[:6], refs[6 : 7 + k], refs[7 + k :]
    total = jnp.zeros((128, 128), F32)
    for c in range(CELLS):
        product = None
        for index, (cell, _, (which, row)) in enumerate(OUTER):
            if cell == c:
                term = w_ref[index] * halo[which][row : row + 1, :]
                product = term if product is None else product + term
        total = place_column(total, jnp.sum(product, axis=1, keepdims=True), c)
    image = jnp.transpose(total)[0:16, :] + part_ref[...]
    diag = diag_ref[...]
    v = basis[k][...]
    new = (image - PER_PARTICLE * v) / diag
    if SHIFT[k]:
        new = new - SHIFT[k] * v
    outs[0][...] = new
    if k < 3:
        write_faces(new, outs[1:5])
    else:
        vectors = [ref[...] for ref in basis] + [new]
        rows = []
        for i in range(4):
            scaled = vectors[i] * diag
            for j in range(i, 5):
                rows.append(jnp.sum(scaled * vectors[j], axis=0, keepdims=True))
        rows.append(jnp.zeros((128 - len(rows), 128), F32))
        lanes = jnp.sum(jnp.transpose(jnp.concatenate(rows, axis=0)), axis=0, keepdims=True)
        outs[1][...] = jnp.broadcast_to(lanes, (8, 128))


def apply_outer(k, part, diag, w, halo, basis):
    if k < 3:
        outs = (shape(16, 128),) + (shape(4, 128),) * 4
    else:
        outs = (shape(16, 128), shape(8, 128))
    return pl.pallas_call(
        functools.partial(outer_kernel, k),
        out_shape=outs,
        in_specs=whole(9 + k + 1),
        out_specs=tuple(whole(len(outs))),
        compiler_params=params(16),
        name="apply_outer",
    )(part, diag, w, *halo, *basis)


def coefficients(sums):
    table = {}
    lane = lax.broadcasted_iota(jnp.int32, (1, 128), 1)
    for index, (i, j) in enumerate(PAIRS):
        one = jnp.sum(jnp.where(lane == index, sums, 0.0), axis=1, keepdims=True)
        table[i, j] = table[j, i] = one
    scale, matrix = [], {}
    for i in range(4):
        for j in range(i + 1):
            one = (1.0 - SHIFT[j]) * table[i, j] - table[i, j + 1]
            if i != j:
                two = (1.0 - SHIFT[i]) * table[j, i] - table[j, i + 1]
                one = 0.5 * (one + two)
            matrix[i, j] = one
    for i in range(4):
        scale.append(lax.rsqrt(jnp.maximum(matrix[i, i], 1e-35)))
    right = [table[i, 0] * scale[i] for i in range(4)]
    lower, pivot = {}, []
    for j in range(4):
        value = matrix[j, j] * scale[j] * scale[j]
        for k in range(j):
            value = value - lower[j, k] * lower[j, k] * pivot[k]
        pivot.append(jnp.maximum(value, 3e-7))
        for i in range(j + 1, 4):
            value = matrix[i, j] * scale[i] * scale[j]
            for k in range(j):
                value = value - lower[i, k] * lower[j, k] * pivot[k]
            lower[i, j] = value / pivot[j]
    for i in range(4):
        for k in range(i):
            right[i] = right[i] - lower[i, k] * right[k]
    right = [right[i] / pivot[i] for i in range(4)]
    for i in reversed(range(4)):
        for k in range(i + 1, 4):
            right[i] = right[i] - lower[k, i] * right[k]
    return [right[i] * scale[i] for i in range(4)]


def advance(total, motion, mass, coefs, lanes):
    lane = lax.broadcasted_iota(jnp.int32, total.shape, 1)
    term = (lane >> 4) & 3
    factor = jnp.zeros(total.shape, F32)
    for k in range(4):
        factor = jnp.where(term == k, coefs[k], factor)
    scaled = jnp.where(lane < lanes, total * factor, 0.0)
    force = scaled
    for k in range(1, 4):
        force = force + pltpu.roll(scaled, 128 - 16 * k, 1)
    velocity = motion + STEP_TIME * force / mass
    moved = motion + STEP_TIME * pltpu.roll(velocity, 16, 1)
    kept = jnp.where(term == 0, velocity, jnp.where(term == 1, moved, 0.0))
    return jnp.where(lane < lanes, kept, 0.0)


def marker_kernel(step, *refs):
    if step == 0:
        codes_ref, recv_ref, feature_ref = refs[:3]
        n_ref, added_ref, rows_ref, moving_ref = refs[3:7]
        scratch = refs[7:]
    else:
        codes_ref, recv_ref, feature_ref, before_ref, diag_ref, payload_ref, motion_ref = refs[:7]
        basis = refs[7:12]
        n_ref, added_ref, first_ref, y0, y3, z0, z3, x_ref, moving_ref = refs[12:21]
        scratch = refs[21:]
    tile_ref, total_ref, even_ref, odd_ref = scratch

    if step == 0:
        moving_ref[0] = recv_ref[:, 49, :]
        moving_ref[1] = recv_ref[:, 50, :]
    else:
        coefs = coefficients(payload_ref[96:97, :])
        mass = recv_ref[:, 51, :]
        part = payload_ref[64:96, :]
        second = jnp.concatenate([part, pltpu.roll(part, 64, 1)], axis=0)
        moving_ref[0] = advance(payload_ref[0:64, :], motion_ref[0], mass, coefs, 128)
        moving_ref[1] = advance(second, motion_ref[1], mass, coefs, 64)

    row = lax.broadcasted_iota(jnp.int32, (8, 128), 0)
    lane = lax.broadcasted_iota(jnp.int32, (8, 128), 1)
    pick = jnp.where(row < 3, row * 4 + 1, jnp.where(row < 6, (row - 3) * 4, 32)) * 16
    scale = jnp.where(row < 3, ROOT, 1.0)

    def spread(s):
        low = jnp.broadcast_to(moving_ref[0, pl.ds(s, 1), :], (8, 128))
        high = jnp.broadcast_to(moving_ref[1, pl.ds(s, 1), :], (8, 128))
        tiles = []
        for r in range(8):
            target = pick + (codes_ref[s * 8 + r] >> 4)
            chosen = jnp.where(lane == target, low, jnp.where(lane + 128 == target, high, 0.0))
            tiles.append(jnp.broadcast_to(jnp.sum(chosen, axis=1, keepdims=True), (8, 128)) * scale)
        for r in range(8):
            tile_ref[s, r] = tiles[r]

    total_ref[...] = jnp.zeros((CELLS, 8, 128), F32)

    def weigh(s, r, buffer_ref):
        c = codes_ref[s * 8 + r] & 15
        place = recv_ref[s, 6 * r : 6 * r + 8, :] + tile_ref[s, r]
        high = place.astype(BF16).astype(F32)
        square = jnp.sum(jnp.where(row < 3, place * place, 0.0), axis=0, keepdims=True)
        square = jnp.broadcast_to(square, (8, 128))
        first = square.astype(BF16).astype(F32)
        second = (square - first).astype(BF16).astype(F32)
        third = square - first - second
        ends = jnp.where(row == 0, first, jnp.where(row == 1, second, jnp.where(row == 2, third, 1.0)))
        right = jnp.concatenate([high, place - high, high, ends], axis=0).astype(BF16)
        power = jnp.dot(feature_ref[c], right, preferred_element_type=F32)
        upper, lower = split2(jnp.exp2(power))
        buffer_ref[r, 0:128, :] = upper
        buffer_ref[r, 128:256, :] = lower

    def contract(s, r, buffer_ref):
        left = jnp.concatenate(split2(recv_ref[s, 6 * r : 6 * r + 8, :]), axis=0)
        both = lax.dot_general(left, buffer_ref[r], NT, preferred_element_type=F32)
        return both[0:8, 0:128] + both[8:16, 0:128] + both[0:8, 128:256]

    def turn(s_next, next_ref, s_now, now_ref):
        results = []
        for r in range(8):
            weigh(s_next, r, next_ref)
            results.append(contract(s_now, r, now_ref))
        for r in range(8):
            c = codes_ref[s_now * 8 + r] & 15
            total_ref[c] = total_ref[c] + results[r] * tile_ref[s_now, r]
            if r % 2 == 1:
                pair = pl.ds(pl.multiple_of(s_now * 32, 32) + 4 * (r - 1), 8)
                below, above = pltpu.roll(results[r - 1], 5, 0), pltpu.roll(results[r], 1, 0)
                n_ref[pair, :] = jnp.where(row < 4, below, above)
                if step == 0:
                    rows_ref[pair, :] = jnp.where(
                        row < 4, codes_ref[s_now * 8 + r - 1], codes_ref[s_now * 8 + r]
                    )
        spread(jnp.minimum(s_next + 1, TILES - 1))

    spread(0)
    for r in range(8):
        weigh(0, r, even_ref)
    spread(1)

    @pl.loop(0, TILES // 2)
    def _(t):
        turn(2 * t + 1, odd_ref, 2 * t, even_ref)
        turn(jnp.minimum(2 * t + 2, TILES - 1), even_ref, 2 * t + 1, odd_ref)

    for c in range(CELLS):
        added_ref[c : c + 1, :] = jnp.sum(total_ref[c][3:6, :], axis=0, keepdims=True)
    if step == 0:
        return
    vectors = [ref[...] for ref in basis]
    x = None
    first = vectors[0] + (added_ref[...] - before_ref[...]) / diag_ref[...]
    for k in range(4):
        term = coefs[k] * vectors[k]
        x = term if x is None else x + term
        first = first - coefs[k] * ((1.0 - SHIFT[k]) * vectors[k] - vectors[k + 1])
    x_ref[...] = x
    first_ref[...] = first
    write_faces(first, (y0, y3, z0, z3))


def marker_pass(step, *args):
    outs = (shape(4 * SLOTS, 128), shape(16, 128))
    if step:
        outs = outs + (shape(16, 128),) + (shape(4, 128),) * 4 + (shape(16, 128),)
    else:
        outs = outs + (shape(4 * SLOTS, 128, dtype=jnp.int32),)
    outs = outs + (shape(2, TILES, 128),)
    return pl.pallas_call(
        functools.partial(marker_kernel, step),
        out_shape=outs,
        in_specs=whole(1, SMEM) + whole(len(args) - 1),
        out_specs=tuple(whole(len(outs))),
        scratch_shapes=[
            VMEM((TILES, 8, 8, 128), F32),
            VMEM((CELLS, 8, 128), F32),
            VMEM((8, 256, 128), BF16),
            VMEM((8, 256, 128), BF16),
        ],
        compiler_params=params(32),
        name="markers",
    )(*args)


def features(own):
    def rounded(x):
        return lax.reduce_precision(x, 8, 7)

    o = (own.reshape(3, CELLS, 128) - 0.5) * ROOT
    high = rounded(2.0 * o)
    middle = rounded(2.0 * o - high)
    square = o[0] * o[0] + o[1] * o[1] + o[2] * o[2]
    first = rounded(square)
    second = rounded(square - first)
    third = square - first - second
    five, two = jnp.zeros((5, CELLS, 128), F32), jnp.zeros((2, CELLS, 128), F32)
    ends = jnp.concatenate([-jnp.ones((3, CELLS, 128), F32), -jnp.stack([first, second, third]), two])
    rows = jnp.concatenate([high, five, high, five, middle, five, ends])
    return jnp.transpose(rows, (1, 2, 0)).astype(BF16)


def force_kernel(n_ref, rows_ref, *refs):
    basis, out_ref, wide_ref = refs[:-2], refs[-2], refs[-1]
    count = len(basis)
    empty = jnp.zeros((16, 128), F32)
    vectors = [ref[...] for ref in basis]
    right_high, right_low = split2(jnp.concatenate(vectors + [empty] * (8 - count), axis=0))
    lane_cell = lax.broadcasted_iota(jnp.int32, (256, 128), 1) & 15
    source = lax.broadcasted_iota(jnp.int32, (128, 256), 0) >> 4
    target = lax.broadcasted_iota(jnp.int32, (128, 256), 1) >> 4
    spread = jnp.where((target % count == source) & (target < 3 * count), 1.0, 0.0).astype(BF16)
    lane = lax.broadcasted_iota(jnp.int32, (256, 256), 1)
    component = lax.broadcasted_iota(jnp.int32, (256, 256), 0) & 3
    fits = (lane >> 4) // count == component
    lane_grain = jnp.where(fits, lane & 15, -1)

    @pl.loop(0, 8)
    def _(chunk):
        rows = pl.ds(pl.multiple_of(chunk * 256, 256), 256)
        high, low = split2(n_ref[rows, :])
        dots = lax.dot_general(high, right_high, NT, preferred_element_type=F32)
        dots = dots + lax.dot_general(low, right_high, NT, preferred_element_type=F32)
        dots = dots + lax.dot_general(high, right_low, NT, preferred_element_type=F32)
        code = rows_ref[rows, :]
        dots = jnp.where(lane_cell == (code & 15), dots, 0.0)
        wide = None
        for piece in split3(dots):
            one = jnp.dot(piece, spread, preferred_element_type=F32)
            wide = one if wide is None else wide + one
        grain = jnp.concatenate([code, code], axis=1) >> 4
        kept = jnp.where(lane_grain == grain, wide, 0.0).reshape(8, 32, 256)
        wide_ref[pl.ds(pl.multiple_of(chunk * 8, 8), 8), :] = jnp.sum(kept, axis=1)

    if count == 4:
        out_ref[0:64, :] = wide_ref[:, 0:128]
        half = lax.broadcasted_iota(jnp.int32, (32, 128), 1) < 64
        below = pltpu.roll(wide_ref[32:64, 128:256], 64, 1)
        out_ref[64:96, :] = jnp.where(half, wide_ref[0:32, 128:256], below)
    else:
        out_ref[...] = wide_ref[...]


def forces(n, rows, basis):
    return pl.pallas_call(
        force_kernel,
        out_shape=shape(96, 128) if len(basis) == 4 else shape(64, 256),
        in_specs=whole(2 + len(basis)),
        out_specs=pl.BlockSpec(memory_space=VMEM),
        scratch_shapes=[VMEM((64, 256), F32)],
        compiler_params=params(32),
        cost_estimate=pl.CostEstimate(flops=4 << 20, bytes_accessed=16 << 20, transcendentals=0),
        name="forces",
    )(n, rows, *basis)


def final_kernel(got_ref, x_ref, *refs):
    basis, (out_ref, scaled_ref) = refs[:4], refs[4:]
    got = [jnp.sum(got_ref[:, h, :], axis=0, keepdims=True) for h in range(3)]
    coefs = coefficients(got[2])
    x = x_ref[...]
    for k in range(4):
        x = x + coefs[k] * basis[k][...]
    out_ref[...] = x
    for h in range(2):
        term = (lax.broadcasted_iota(jnp.int32, (1, 128), 1) // 16 + 8 * h) % 5
        factor = jnp.ones((1, 128), F32)
        for k in range(4):
            factor = jnp.where(term == k + 1, coefs[k], factor)
        scaled_ref[h : h + 1, :] = got[h] * factor


def final(got, x, basis):
    return pl.pallas_call(
        final_kernel,
        out_shape=(shape(16, 128), shape(2, 128)),
        in_specs=whole(6),
        out_specs=tuple(whole(2)),
        compiler_params=params(16),
        name="final",
    )(got, x, *basis)


def ring(x, axis, by):
    n = lax.axis_size(axis)
    return lax.ppermute(x, axis, [(i, (i + by) % n) for i in range(n)])


def halo_of(v, y0, y3, z0, z3):
    return (
        ring(v, "flow", -1),
        ring(v, "flow", 1),
        ring(y0, "cross", -1),
        ring(y3, "cross", 1),
        ring(z0, "depth", -1),
        ring(z3, "depth", 1),
    )


def exchange_sum(x, axes):
    for axis in axes:
        n = lax.axis_size(axis)
        m = 1
        while m < n:
            x = x + lax.ppermute(x, axis, [(i, i ^ m) for i in range(n)])
            m *= 2
    return x


def per_device(
    fluid_offsets,
    source,
    marker_offsets,
    marker_normals,
    dest_tile,
    cell_index,
    grain_velocity,
    grain_mass,
):
    source = source.reshape(16, 128)
    offs = fluid_offsets.reshape(3, 4, 4, 128)
    own = offs.reshape(48, 128)
    lanes = jnp.pad(jnp.transpose(grain_velocity), ((0, 1), (0, 48))).reshape(2, 128)
    mass = jnp.broadcast_to(grain_mass[None, :], (8, 16)).reshape(1, 128)
    meta = jnp.concatenate([jnp.zeros((1, 128), F32), lanes, mass, jnp.zeros((4, 128), F32)])
    packed = pack(
        dest_tile.reshape(16, 16),
        cell_index,
        jnp.transpose(marker_offsets, (0, 2, 1, 3)),
        jnp.transpose(marker_normals, (0, 2, 1, 3)),
        meta,
    )
    recv = lax.all_to_all(packed, ("flow", "cross"), split_axis=0, concat_axis=0, tiled=True)
    halo = halo_of(
        own,
        offs[:, 0].reshape(12, 128),
        offs[:, 3].reshape(12, 128),
        offs[:, :, 0].reshape(12, 128),
        offs[:, :, 3].reshape(12, 128),
    )
    feature = features(own)
    codes = recv[:, 48, 0:8].astype(jnp.int32).reshape(SLOTS)

    x = None
    n = rows = motion = added = basis = payload = None
    for step in range(STEPS):
        if step == 0:
            n, added, rows, motion = marker_pass(0, codes, recv, feature)
            w_inner, w_outer, diag, v, *faces = weights(own, source, added, halo)
        else:
            n, added, v, *rest = marker_pass(
                1, codes, recv, feature, added, diag, payload, motion, *basis
            )
            faces, x, motion = rest[:4], rest[4], rest[5]
        basis = [v]
        for k in range(4):
            halo = halo_of(basis[k], *faces)
            part = apply_inner(basis[k], w_inner)
            v, *faces = apply_outer(k, part, diag, w_outer, halo, basis)
            basis.append(v)
        sums = exchange_sum(faces[0], ("depth",))
        if step < STEPS - 1:
            felt = forces(n, rows, basis[:4])
            payload = exchange_sum(jnp.concatenate([felt, sums]), ("flow", "cross"))
    felt = forces(n, rows, [x] + basis[:4]).reshape(TILES, 2, 128)
    send = jnp.concatenate([felt, jnp.broadcast_to(sums[0:1], (TILES, 1, 128))], axis=1)
    got = lax.all_to_all(send, ("flow", "cross"), split_axis=0, concat_axis=0, tiled=True)
    pressure, scaled = final(got, x, basis[:4])
    force = jnp.sum(scaled.reshape(256)[:240].reshape(3, 5, 16), axis=1)
    index = lax.axis_index("flow") * lax.axis_size("cross") + lax.axis_index("cross")
    mine = lax.dynamic_slice_in_dim(motion, index, 1, axis=1).reshape(4, 64)[:3, :16]
    velocity = jnp.transpose(mine + STEP_TIME * force / grain_mass[None, :])
    return pressure.reshape(1, 4, 4, 128), velocity


def solution(mesh):
    owners = ("flow", "cross", "depth")
    return jax.shard_map(
        per_device,
        mesh=mesh,
        in_specs=(
            P(None, "flow", "cross", "depth", None),
            P("flow", "cross", "depth", None),
            P(owners, None, None, None),
            P(owners, None, None, None),
            P(owners, None, None),
            P(owners, None),
            P(owners, None),
            P(owners),
        ),
        out_specs=(P("flow", "cross", "depth", None), P(owners, None)),
        check_vma=False,
    )
```

```python
import functools

import jax
import jax.numpy as jnp
from jax import lax
from jax.experimental import pallas as pl
from jax.experimental.pallas import tpu as pltpu
from jax.sharding import PartitionSpec as P

STEPS = 2
STIFFEN = 0.5
STEP_TIME = 0.05
PER_PARTICLE = 1.0 / 128.0
ROOT = 1.2011224087864498
SHIFT = (0.0, 0.7, 0.3, 0.5)
CELLS = 16
SLOTS = 512
TILES = 64
CAP = 8
F32 = jnp.float32
BF16 = jnp.bfloat16
VMEM = pltpu.VMEM
SMEM = pltpu.SMEM
NT = (((1,), (1,)), ((), ()))
PAIRS = tuple((i, j) for i in range(4) for j in range(i, 5))


def params(mib):
    return pltpu.CompilerParams(vmem_limit_bytes=mib * 1024 * 1024)


def whole(count, space=VMEM):
    return [pl.BlockSpec(memory_space=space)] * count


def shape(*dims, dtype=F32):
    return jax.ShapeDtypeStruct(dims, dtype)


def inner_pairs():
    out = []
    for c in range(CELLS):
        y, z = c // 4, c % 4
        out.append((c, (0, 0, 0), c))
        if y < 3:
            out.append((c, (0, 1, 0), c + 4))
        if y > 0:
            out.append((c, (0, -1, 0), c - 4))
        if z < 3:
            out.append((c, (0, 0, 1), c + 1))
        if z > 0:
            out.append((c, (0, 0, -1), c - 1))
    return out


def outer_pairs():
    out = []
    for c in range(CELLS):
        y, z = c // 4, c % 4
        out.append((c, (1, 0, 0), (0, c)))
        out.append((c, (-1, 0, 0), (1, c)))
        if y == 3:
            out.append((c, (0, 1, 0), (2, z)))
        if y == 0:
            out.append((c, (0, -1, 0), (3, z)))
        if z == 3:
            out.append((c, (0, 0, 1), (4, y)))
        if z == 0:
            out.append((c, (0, 0, -1), (5, y)))
    return out


INNER = inner_pairs()
OUTER = outer_pairs()


def split2(x):
    high = x.astype(BF16)
    return high, (x - high.astype(F32)).astype(BF16)


def split3(x):
    high = x.astype(BF16)
    rest = x - high.astype(F32)
    middle = rest.astype(BF16)
    return high, middle, (rest - middle.astype(F32)).astype(BF16)


def place_column(total, column, c):
    lane = lax.broadcasted_iota(jnp.int32, (128, 128), 1)
    return jnp.where(lane == c, column, total)


def write_faces(v, faces):
    y0, y3, z0, z3 = faces
    y0[...] = v[0:4, :]
    y3[...] = v[12:16, :]
    for y in range(4):
        z0[y : y + 1, :] = v[4 * y : 4 * y + 1, :]
        z3[y : y + 1, :] = v[4 * y + 3 : 4 * y + 4, :]


def pack_kernel(dest_ref, cell_ref, velocity_ref, mass_ref, off_ref, nor_ref, buf_ref, count_ref):
    buf_ref[:, 0:48, :] = jnp.zeros((TILES, 48, 128), F32)
    row = lax.broadcasted_iota(jnp.int32, (8, 128), 0)
    place = lax.broadcasted_iota(jnp.int32, (8, 128), 1)
    meta = jnp.zeros((8, 128), F32)
    for g in range(16):
        for a in range(3):
            here = (row == 1 + a // 2) & (place == 64 * (a % 2) + g)
            meta = jnp.where(here, velocity_ref[a, g], meta)
        meta = jnp.where((row == 3) & ((place & 15) == g), mass_ref[g], meta)

    @pl.loop(0, TILES)
    def _(t):
        buf_ref[t, 48:56, :] = meta
        count_ref[t] = 0

    lane = lax.broadcasted_iota(jnp.int32, (1, 128), 1)

    @pl.loop(0, 16)
    def _(g):
        off = [(off_ref[g, a] - 0.5) * ROOT for a in range(3)]
        nor = [nor_ref[g, a] * PER_PARTICLE for a in range(3)]
        for b in range(16):
            d = dest_ref[g, b]
            r = count_ref[d]
            count_ref[d] = r + 1
            for a in range(3):
                buf_ref[d, pl.ds(6 * r + a, 1), :] = off[a][b : b + 1, :]
                buf_ref[d, pl.ds(6 * r + 3 + a, 1), :] = nor[a][b : b + 1, :]
            code = (cell_ref[g, b] + 16 * g).astype(F32)
            buf_ref[d, 48:49, :] = jnp.where(lane == r, code, buf_ref[d, 48:49, :])


def pack(dest, cell, velocity, mass, off, nor):
    return pl.pallas_call(
        pack_kernel,
        out_shape=shape(TILES, 56, 128),
        in_specs=whole(4, SMEM) + whole(2),
        out_specs=pl.BlockSpec(memory_space=VMEM),
        scratch_shapes=[SMEM((TILES,), jnp.int32)],
        compiler_params=params(56),
        cost_estimate=pl.CostEstimate(flops=4 << 20, bytes_accessed=16 << 20, transcendentals=0),
        name="pack",
    )(dest, cell, velocity, mass, off, nor)


def weights_kernel(own_ref, source_ref, added_ref, *refs):
    halo, (inner_ref, outer_ref, diag_ref, first_ref, *faces) = refs[:6], refs[6:]
    own = own_ref[...] * ROOT
    columns = jnp.transpose(jnp.concatenate([own, jnp.zeros((80, 128), F32)], axis=0))
    total = jnp.zeros((128, 128), F32)
    inner, outer = list(enumerate(INNER)), list(enumerate(OUTER))
    for c in range(CELLS):
        mine = [columns[:, 16 * a + c : 16 * a + c + 1] for a in range(3)]
        rowsum = jnp.zeros((128, 128), F32)
        for index, (_, step, near) in [p for p in inner if p[1][0] == c]:
            square = None
            for a in range(3):
                gap = (own[16 * a + near : 16 * a + near + 1, :] + step[a] * ROOT) - mine[a]
                square = gap * gap if square is None else square + gap * gap
            weight = jnp.exp2(-square) * PER_PARTICLE
            inner_ref[index] = weight
            rowsum = rowsum + weight
        for index, (_, step, (which, row)) in [p for p in outer if p[1][0] == c]:
            count = 16 if which < 2 else 4
            square = None
            for a in range(3):
                at = count * a + row
                gap = (halo[which][at : at + 1, :] * ROOT + step[a] * ROOT) - mine[a]
                square = gap * gap if square is None else square + gap * gap
            weight = jnp.exp2(-square) * PER_PARTICLE
            outer_ref[index] = weight
            rowsum = rowsum + weight
        total = place_column(total, jnp.sum(rowsum, axis=1, keepdims=True), c)
    diag = jnp.transpose(total)[0:16, :] + (STIFFEN - PER_PARTICLE)
    diag_ref[...] = diag
    first = (source_ref[...] + added_ref[...]) / diag
    first_ref[...] = first
    write_faces(first, faces)


def weights(own, source, added, halo):
    outs = (shape(len(INNER), 128, 128), shape(len(OUTER), 128, 128), shape(16, 128), shape(16, 128))
    return pl.pallas_call(
        weights_kernel,
        out_shape=outs + (shape(4, 128),) * 4,
        in_specs=whole(9),
        out_specs=tuple(whole(8)),
        compiler_params=params(32),
        name="weights",
    )(own, source, added, *halo)


def inner_kernel(v_ref, w_ref, out_ref):
    total = jnp.zeros((128, 128), F32)
    for c in range(CELLS):
        product = None
        for index, (cell, _, near) in enumerate(INNER):
            if cell == c:
                term = w_ref[index] * v_ref[near : near + 1, :]
                product = term if product is None else product + term
        total = place_column(total, jnp.sum(product, axis=1, keepdims=True), c)
    out_ref[...] = jnp.transpose(total)[0:16, :]


def apply_inner(v, w):
    return pl.pallas_call(
        inner_kernel,
        out_shape=shape(16, 128),
        in_specs=whole(2),
        out_specs=pl.BlockSpec(memory_space=VMEM),
        compiler_params=params(16),
        cost_estimate=pl.CostEstimate(flops=4 << 20, bytes_accessed=5 << 20, transcendentals=0),
        name="apply_inner",
    )(v, w)


def outer_kernel(k, part_ref, diag_ref, w_ref, *refs):
    halo, basis, outs = refs[:6], refs[6 : 7 + k], refs[7 + k :]
    total = jnp.zeros((128, 128), F32)
    for c in range(CELLS):
        product = None
        for index, (cell, _, (which, row)) in enumerate(OUTER):
            if cell == c:
                term = w_ref[index] * halo[which][row : row + 1, :]
                product = term if product is None else product + term
        total = place_column(total, jnp.sum(product, axis=1, keepdims=True), c)
    image = jnp.transpose(total)[0:16, :] + part_ref[...]
    diag = diag_ref[...]
    v = basis[k][...]
    new = (image - PER_PARTICLE * v) / diag
    if SHIFT[k]:
        new = new - SHIFT[k] * v
    outs[0][...] = new
    if k < 3:
        write_faces(new, outs[1:5])
    else:
        vectors = [ref[...] for ref in basis] + [new]
        rows = []
        for i in range(4):
            scaled = vectors[i] * diag
            for j in range(i, 5):
                rows.append(jnp.sum(scaled * vectors[j], axis=0, keepdims=True))
        rows.append(jnp.zeros((128 - len(rows), 128), F32))
        lanes = jnp.sum(jnp.transpose(jnp.concatenate(rows, axis=0)), axis=0, keepdims=True)
        outs[1][...] = jnp.broadcast_to(lanes, (8, 128))


def apply_outer(k, part, diag, w, halo, basis):
    if k < 3:
        outs = (shape(16, 128),) + (shape(4, 128),) * 4
    else:
        outs = (shape(16, 128), shape(8, 128))
    return pl.pallas_call(
        functools.partial(outer_kernel, k),
        out_shape=outs,
        in_specs=whole(9 + k + 1),
        out_specs=tuple(whole(len(outs))),
        compiler_params=params(16),
        name="apply_outer",
    )(part, diag, w, *halo, *basis)


def coefficients(sums):
    table = {}
    lane = lax.broadcasted_iota(jnp.int32, (1, 128), 1)
    for index, (i, j) in enumerate(PAIRS):
        one = jnp.sum(jnp.where(lane == index, sums, 0.0), axis=1, keepdims=True)
        table[i, j] = table[j, i] = one
    scale, matrix = [], {}
    for i in range(4):
        for j in range(i + 1):
            one = (1.0 - SHIFT[j]) * table[i, j] - table[i, j + 1]
            if i != j:
                two = (1.0 - SHIFT[i]) * table[j, i] - table[j, i + 1]
                one = 0.5 * (one + two)
            matrix[i, j] = one
    for i in range(4):
        scale.append(lax.rsqrt(jnp.maximum(matrix[i, i], 1e-35)))
    right = [table[i, 0] * scale[i] for i in range(4)]
    lower, pivot = {}, []
    for j in range(4):
        value = matrix[j, j] * scale[j] * scale[j]
        for k in range(j):
            value = value - lower[j, k] * lower[j, k] * pivot[k]
        pivot.append(jnp.maximum(value, 3e-7))
        for i in range(j + 1, 4):
            value = matrix[i, j] * scale[i] * scale[j]
            for k in range(j):
                value = value - lower[i, k] * lower[j, k] * pivot[k]
            lower[i, j] = value / pivot[j]
    for i in range(4):
        for k in range(i):
            right[i] = right[i] - lower[i, k] * right[k]
    right = [right[i] / pivot[i] for i in range(4)]
    for i in reversed(range(4)):
        for k in range(i + 1, 4):
            right[i] = right[i] - lower[k, i] * right[k]
    return [right[i] * scale[i] for i in range(4)]


def advance(total, motion, mass, coefs, lanes):
    lane = lax.broadcasted_iota(jnp.int32, total.shape, 1)
    term = (lane >> 4) & 3
    factor = jnp.zeros(total.shape, F32)
    for k in range(4):
        factor = jnp.where(term == k, coefs[k], factor)
    scaled = jnp.where(lane < lanes, total * factor, 0.0)
    force = scaled
    for k in range(1, 4):
        force = force + pltpu.roll(scaled, 128 - 16 * k, 1)
    velocity = motion + STEP_TIME * force / mass
    moved = motion + STEP_TIME * pltpu.roll(velocity, 16, 1)
    kept = jnp.where(term == 0, velocity, jnp.where(term == 1, moved, 0.0))
    return jnp.where(lane < lanes, kept, 0.0)


def marker_kernel(step, *refs):
    if step == 0:
        codes_ref, recv_ref, feature_ref = refs[:3]
        n_ref, added_ref, rows_ref, moving_ref = refs[3:7]
        scratch = refs[7:]
    else:
        codes_ref, recv_ref, feature_ref, before_ref, diag_ref, payload_ref, motion_ref = refs[:7]
        basis = refs[7:12]
        n_ref, added_ref, first_ref, y0, y3, z0, z3, x_ref, moving_ref = refs[12:21]
        scratch = refs[21:]
    tile_ref, total_ref, even_ref, odd_ref = scratch

    if step == 0:
        moving_ref[0] = recv_ref[:, 49, :]
        moving_ref[1] = recv_ref[:, 50, :]
    else:
        coefs = coefficients(payload_ref[96:97, :])
        mass = recv_ref[:, 51, :]
        part = payload_ref[64:96, :]
        second = jnp.concatenate([part, pltpu.roll(part, 64, 1)], axis=0)
        moving_ref[0] = advance(payload_ref[0:64, :], motion_ref[0], mass, coefs, 128)
        moving_ref[1] = advance(second, motion_ref[1], mass, coefs, 64)

    row = lax.broadcasted_iota(jnp.int32, (8, 128), 0)
    lane = lax.broadcasted_iota(jnp.int32, (8, 128), 1)
    pick = jnp.where(row < 3, row * 4 + 1, jnp.where(row < 6, (row - 3) * 4, 32)) * 16
    scale = jnp.where(row < 3, ROOT, 1.0)

    def spread(s):
        low = jnp.broadcast_to(moving_ref[0, pl.ds(s, 1), :], (8, 128))
        high = jnp.broadcast_to(moving_ref[1, pl.ds(s, 1), :], (8, 128))
        tiles = []
        for r in range(8):
            target = pick + (codes_ref[s * 8 + r] >> 4)
            chosen = jnp.where(lane == target, low, jnp.where(lane + 128 == target, high, 0.0))
            tiles.append(jnp.broadcast_to(jnp.sum(chosen, axis=1, keepdims=True), (8, 128)) * scale)
        for r in range(8):
            tile_ref[s, r] = tiles[r]

    total_ref[...] = jnp.zeros((CELLS, 8, 128), F32)

    def weigh(s, r, buffer_ref):
        c = codes_ref[s * 8 + r] & 15
        place = recv_ref[s, 6 * r : 6 * r + 8, :] + tile_ref[s, r]
        high = place.astype(BF16).astype(F32)
        square = jnp.sum(jnp.where(row < 3, place * place, 0.0), axis=0, keepdims=True)
        square = jnp.broadcast_to(square, (8, 128))
        first = square.astype(BF16).astype(F32)
        second = (square - first).astype(BF16).astype(F32)
        third = square - first - second
        ends = jnp.where(row == 0, first, jnp.where(row == 1, second, jnp.where(row == 2, third, 1.0)))
        right = jnp.concatenate([high, place - high, high, ends], axis=0).astype(BF16)
        power = jnp.dot(feature_ref[c], right, preferred_element_type=F32)
        upper, lower = split2(jnp.exp2(power))
        buffer_ref[r, 0:128, :] = upper
        buffer_ref[r, 128:256, :] = lower

    def contract(s, r, buffer_ref):
        left = jnp.concatenate(split2(recv_ref[s, 6 * r : 6 * r + 8, :]), axis=0)
        both = lax.dot_general(left, buffer_ref[r], NT, preferred_element_type=F32)
        return both[0:8, 0:128] + both[8:16, 0:128] + both[0:8, 128:256]

    def turn(s_next, next_ref, s_now, now_ref):
        results = []
        for r in range(8):
            weigh(s_next, r, next_ref)
            results.append(contract(s_now, r, now_ref))
        for r in range(8):
            c = codes_ref[s_now * 8 + r] & 15
            total_ref[c] = total_ref[c] + results[r] * tile_ref[s_now, r]
            if r % 2 == 1:
                pair = pl.ds(pl.multiple_of(s_now * 32, 32) + 4 * (r - 1), 8)
                below, above = pltpu.roll(results[r - 1], 5, 0), pltpu.roll(results[r], 1, 0)
                n_ref[pair, :] = jnp.where(row < 4, below, above)
                if step == 0:
                    rows_ref[pair, :] = jnp.where(
                        row < 4, codes_ref[s_now * 8 + r - 1], codes_ref[s_now * 8 + r]
                    )
        spread(jnp.minimum(s_next + 1, TILES - 1))

    spread(0)
    for r in range(8):
        weigh(0, r, even_ref)
    spread(1)

    @pl.loop(0, TILES // 2)
    def _(t):
        turn(2 * t + 1, odd_ref, 2 * t, even_ref)
        turn(jnp.minimum(2 * t + 2, TILES - 1), even_ref, 2 * t + 1, odd_ref)

    for c in range(CELLS):
        added_ref[c : c + 1, :] = jnp.sum(total_ref[c][3:6, :], axis=0, keepdims=True)
    if step == 0:
        return
    vectors = [ref[...] for ref in basis]
    x = None
    first = vectors[0] + (added_ref[...] - before_ref[...]) / diag_ref[...]
    for k in range(4):
        term = coefs[k] * vectors[k]
        x = term if x is None else x + term
        first = first - coefs[k] * ((1.0 - SHIFT[k]) * vectors[k] - vectors[k + 1])
    x_ref[...] = x
    first_ref[...] = first
    write_faces(first, (y0, y3, z0, z3))


def marker_pass(step, *args):
    outs = (shape(4 * SLOTS, 128), shape(16, 128))
    if step:
        outs = outs + (shape(16, 128),) + (shape(4, 128),) * 4 + (shape(16, 128),)
    else:
        outs = outs + (shape(4 * SLOTS, 128, dtype=jnp.int32),)
    outs = outs + (shape(2, TILES, 128),)
    return pl.pallas_call(
        functools.partial(marker_kernel, step),
        out_shape=outs,
        in_specs=whole(1, SMEM) + whole(len(args) - 1),
        out_specs=tuple(whole(len(outs))),
        scratch_shapes=[
            VMEM((TILES, 8, 8, 128), F32),
            VMEM((CELLS, 8, 128), F32),
            VMEM((8, 256, 128), BF16),
            VMEM((8, 256, 128), BF16),
        ],
        compiler_params=params(32),
        name="markers",
    )(*args)


def features(own):
    def rounded(x):
        return lax.reduce_precision(x, 8, 7)

    o = (own.reshape(3, CELLS, 128) - 0.5) * ROOT
    high = rounded(2.0 * o)
    middle = rounded(2.0 * o - high)
    square = o[0] * o[0] + o[1] * o[1] + o[2] * o[2]
    first = rounded(square)
    second = rounded(square - first)
    third = square - first - second
    five, two = jnp.zeros((5, CELLS, 128), F32), jnp.zeros((2, CELLS, 128), F32)
    ends = jnp.concatenate([-jnp.ones((3, CELLS, 128), F32), -jnp.stack([first, second, third]), two])
    rows = jnp.concatenate([high, five, high, five, middle, five, ends])
    return jnp.transpose(rows, (1, 2, 0)).astype(BF16)


def force_kernel(n_ref, rows_ref, *refs):
    basis, out_ref, wide_ref = refs[:-2], refs[-2], refs[-1]
    count = len(basis)
    empty = jnp.zeros((16, 128), F32)
    vectors = [ref[...] for ref in basis]
    right_high, right_low = split2(jnp.concatenate(vectors + [empty] * (8 - count), axis=0))
    lane_cell = lax.broadcasted_iota(jnp.int32, (256, 128), 1) & 15
    source = lax.broadcasted_iota(jnp.int32, (128, 256), 0) >> 4
    target = lax.broadcasted_iota(jnp.int32, (128, 256), 1) >> 4
    spread = jnp.where((target % count == source) & (target < 3 * count), 1.0, 0.0).astype(BF16)
    lane = lax.broadcasted_iota(jnp.int32, (256, 256), 1)
    component = lax.broadcasted_iota(jnp.int32, (256, 256), 0) & 3
    fits = (lane >> 4) // count == component
    lane_grain = jnp.where(fits, lane & 15, -1)

    @pl.loop(0, 8)
    def _(chunk):
        rows = pl.ds(pl.multiple_of(chunk * 256, 256), 256)
        high, low = split2(n_ref[rows, :])
        dots = lax.dot_general(high, right_high, NT, preferred_element_type=F32)
        dots = dots + lax.dot_general(low, right_high, NT, preferred_element_type=F32)
        dots = dots + lax.dot_general(high, right_low, NT, preferred_element_type=F32)
        code = rows_ref[rows, :]
        dots = jnp.where(lane_cell == (code & 15), dots, 0.0)
        wide = None
        for piece in split3(dots):
            one = jnp.dot(piece, spread, preferred_element_type=F32)
            wide = one if wide is None else wide + one
        grain = jnp.concatenate([code, code], axis=1) >> 4
        kept = jnp.where(lane_grain == grain, wide, 0.0).reshape(8, 32, 256)
        wide_ref[pl.ds(pl.multiple_of(chunk * 8, 8), 8), :] = jnp.sum(kept, axis=1)

    if count == 4:
        out_ref[0:64, :] = wide_ref[:, 0:128]
        half = lax.broadcasted_iota(jnp.int32, (32, 128), 1) < 64
        below = pltpu.roll(wide_ref[32:64, 128:256], 64, 1)
        out_ref[64:96, :] = jnp.where(half, wide_ref[0:32, 128:256], below)
    else:
        out_ref[...] = wide_ref[...]


def forces(n, rows, basis):
    return pl.pallas_call(
        force_kernel,
        out_shape=shape(96, 128) if len(basis) == 4 else shape(64, 256),
        in_specs=whole(2 + len(basis)),
        out_specs=pl.BlockSpec(memory_space=VMEM),
        scratch_shapes=[VMEM((64, 256), F32)],
        compiler_params=params(32),
        cost_estimate=pl.CostEstimate(flops=4 << 20, bytes_accessed=16 << 20, transcendentals=0),
        name="forces",
    )(n, rows, *basis)


def final_kernel(got_ref, x_ref, *refs):
    basis, (out_ref, scaled_ref) = refs[:4], refs[4:]
    got = [jnp.sum(got_ref[:, h, :], axis=0, keepdims=True) for h in range(3)]
    coefs = coefficients(got[2])
    x = x_ref[...]
    for k in range(4):
        x = x + coefs[k] * basis[k][...]
    out_ref[...] = x
    for h in range(2):
        term = (lax.broadcasted_iota(jnp.int32, (1, 128), 1) // 16 + 8 * h) % 5
        factor = jnp.ones((1, 128), F32)
        for k in range(4):
            factor = jnp.where(term == k + 1, coefs[k], factor)
        scaled_ref[h : h + 1, :] = got[h] * factor


def final(got, x, basis):
    return pl.pallas_call(
        final_kernel,
        out_shape=(shape(16, 128), shape(2, 128)),
        in_specs=whole(6),
        out_specs=tuple(whole(2)),
        compiler_params=params(16),
        name="final",
    )(got, x, *basis)


def ring(x, axis, by):
    n = lax.axis_size(axis)
    return lax.ppermute(x, axis, [(i, (i + by) % n) for i in range(n)])


def halo_of(v, y0, y3, z0, z3):
    return (
        ring(v, "flow", -1),
        ring(v, "flow", 1),
        ring(y0, "cross", -1),
        ring(y3, "cross", 1),
        ring(z0, "depth", -1),
        ring(z3, "depth", 1),
    )


def exchange_sum(x, axes):
    for axis in axes:
        n = lax.axis_size(axis)
        m = 1
        while m < n:
            x = x + lax.ppermute(x, axis, [(i, i ^ m) for i in range(n)])
            m *= 2
    return x


def per_device(
    fluid_offsets,
    source,
    marker_offsets,
    marker_normals,
    dest_tile,
    cell_index,
    grain_velocity,
    grain_mass,
):
    source = source.reshape(16, 128)
    offs = fluid_offsets.reshape(3, 4, 4, 128)
    own = offs.reshape(48, 128)
    packed = pack(
        dest_tile.reshape(16, 16),
        cell_index,
        jnp.transpose(grain_velocity),
        grain_mass,
        jnp.transpose(marker_offsets, (0, 2, 1, 3)),
        jnp.transpose(marker_normals, (0, 2, 1, 3)),
    )
    recv = lax.all_to_all(packed, ("flow", "cross"), split_axis=0, concat_axis=0, tiled=True)
    halo = halo_of(
        own,
        offs[:, 0].reshape(12, 128),
        offs[:, 3].reshape(12, 128),
        offs[:, :, 0].reshape(12, 128),
        offs[:, :, 3].reshape(12, 128),
    )
    feature = features(own)
    codes = recv[:, 48, 0:8].astype(jnp.int32).reshape(SLOTS)

    x = None
    n = rows = motion = added = basis = payload = None
    for step in range(STEPS):
        if step == 0:
            n, added, rows, motion = marker_pass(0, codes, recv, feature)
            w_inner, w_outer, diag, v, *faces = weights(own, source, added, halo)
        else:
            n, added, v, *rest = marker_pass(
                1, codes, recv, feature, added, diag, payload, motion, *basis
            )
            faces, x, motion = rest[:4], rest[4], rest[5]
        basis = [v]
        for k in range(4):
            halo = halo_of(basis[k], *faces)
            part = apply_inner(basis[k], w_inner)
            v, *faces = apply_outer(k, part, diag, w_outer, halo, basis)
            basis.append(v)
        sums = sum([ring(faces[0], "depth", by) for by in range(1, lax.axis_size("depth"))], faces[0])
        if step < STEPS - 1:
            felt = forces(n, rows, basis[:4])
            payload = exchange_sum(jnp.concatenate([felt, sums]), ("flow", "cross"))
    felt = forces(n, rows, [x] + basis[:4]).reshape(TILES, 2, 128)
    send = jnp.concatenate([felt, jnp.broadcast_to(sums[0:1], (TILES, 1, 128))], axis=1)
    got = lax.all_to_all(send, ("flow", "cross"), split_axis=0, concat_axis=0, tiled=True)
    pressure, scaled = final(got, x, basis[:4])
    force = jnp.sum(scaled.reshape(256)[:240].reshape(3, 5, 16), axis=1)
    index = lax.axis_index("flow") * lax.axis_size("cross") + lax.axis_index("cross")
    mine = lax.dynamic_slice_in_dim(motion, index, 1, axis=1).reshape(4, 64)[:3, :16]
    velocity = jnp.transpose(mine + STEP_TIME * force / grain_mass[None, :])
    return pressure.reshape(1, 4, 4, 128), velocity


def solution(mesh):
    owners = ("flow", "cross", "depth")
    return jax.shard_map(
        per_device,
        mesh=mesh,
        in_specs=(
            P(None, "flow", "cross", "depth", None),
            P("flow", "cross", "depth", None),
            P(owners, None, None, None),
            P(owners, None, None, None),
            P(owners, None, None),
            P(owners, None),
            P(owners, None),
            P(owners),
        ),
        out_specs=(P("flow", "cross", "depth", None), P(owners, None)),
        check_vma=False,
    )
```

```python
import functools

import jax
import jax.numpy as jnp
from jax import lax
from jax.experimental import pallas as pl
from jax.experimental.pallas import tpu as pltpu
from jax.sharding import PartitionSpec as P

STEPS = 2
STIFFEN = 0.5
STEP_TIME = 0.05
PER_PARTICLE = 1.0 / 128.0
ROOT = 1.2011224087864498
SHIFT = (0.0, 0.7, 0.3, 0.5)
CELLS = 16
SLOTS = 512
TILES = 64
CAP = 8
F32 = jnp.float32
BF16 = jnp.bfloat16
VMEM = pltpu.VMEM
SMEM = pltpu.SMEM
NT = (((1,), (1,)), ((), ()))
PAIRS = tuple((i, j) for i in range(4) for j in range(i, 5))


def params(mib):
    return pltpu.CompilerParams(vmem_limit_bytes=mib * 1024 * 1024)


def whole(count, space=VMEM):
    return [pl.BlockSpec(memory_space=space)] * count


def shape(*dims, dtype=F32):
    return jax.ShapeDtypeStruct(dims, dtype)


def inner_pairs():
    out = []
    for c in range(CELLS):
        y, z = c // 4, c % 4
        out.append((c, (0, 0, 0), c))
        if y < 3:
            out.append((c, (0, 1, 0), c + 4))
        if y > 0:
            out.append((c, (0, -1, 0), c - 4))
        if z < 3:
            out.append((c, (0, 0, 1), c + 1))
        if z > 0:
            out.append((c, (0, 0, -1), c - 1))
    return out


def outer_pairs():
    out = []
    for c in range(CELLS):
        y, z = c // 4, c % 4
        out.append((c, (1, 0, 0), (0, c)))
        out.append((c, (-1, 0, 0), (1, c)))
        if y == 3:
            out.append((c, (0, 1, 0), (2, z)))
        if y == 0:
            out.append((c, (0, -1, 0), (3, z)))
        if z == 3:
            out.append((c, (0, 0, 1), (4, y)))
        if z == 0:
            out.append((c, (0, 0, -1), (5, y)))
    return out


INNER = inner_pairs()
OUTER = outer_pairs()


def split2(x):
    high = x.astype(BF16)
    return high, (x - high.astype(F32)).astype(BF16)


def split3(x):
    high = x.astype(BF16)
    rest = x - high.astype(F32)
    middle = rest.astype(BF16)
    return high, middle, (rest - middle.astype(F32)).astype(BF16)


def place_column(total, column, c):
    lane = lax.broadcasted_iota(jnp.int32, (128, 128), 1)
    return jnp.where(lane == c, column, total)


def write_faces(v, faces):
    y0, y3, z0, z3 = faces
    y0[...] = v[0:4, :]
    y3[...] = v[12:16, :]
    for y in range(4):
        z0[y : y + 1, :] = v[4 * y : 4 * y + 1, :]
        z3[y : y + 1, :] = v[4 * y + 3 : 4 * y + 4, :]


def pack_kernel(dest_ref, cell_ref, velocity_ref, mass_ref, off_ref, nor_ref, buf_ref, count_ref):
    buf_ref[:, 0:48, :] = jnp.zeros((TILES, 48, 128), F32)
    row = lax.broadcasted_iota(jnp.int32, (8, 128), 0)
    place = lax.broadcasted_iota(jnp.int32, (8, 128), 1)
    meta = jnp.zeros((8, 128), F32)
    for g in range(16):
        for a in range(3):
            here = (row == 1 + a // 2) & (place == 64 * (a % 2) + g)
            meta = jnp.where(here, velocity_ref[a, g], meta)
        meta = jnp.where((row == 3) & ((place & 15) == g), mass_ref[g], meta)

    @pl.loop(0, TILES)
    def _(t):
        buf_ref[t, 48:56, :] = meta
        count_ref[t] = 0

    lane = lax.broadcasted_iota(jnp.int32, (1, 128), 1)

    @pl.loop(0, 16)
    def _(g):
        off = [(off_ref[g, a] - 0.5) * ROOT for a in range(3)]
        nor = [nor_ref[g, a] * PER_PARTICLE for a in range(3)]
        for b in range(16):
            d = dest_ref[g, b]
            r = count_ref[d]
            count_ref[d] = r + 1
            for a in range(3):
                buf_ref[d, pl.ds(6 * r + a, 1), :] = off[a][b : b + 1, :]
                buf_ref[d, pl.ds(6 * r + 3 + a, 1), :] = nor[a][b : b + 1, :]
            code = (cell_ref[g, b] + 16 * g).astype(F32)
            buf_ref[d, 48:49, :] = jnp.where(lane == r, code, buf_ref[d, 48:49, :])


def pack(dest, cell, velocity, mass, off, nor):
    return pl.pallas_call(
        pack_kernel,
        out_shape=shape(TILES, 56, 128),
        in_specs=whole(4, SMEM) + whole(2),
        out_specs=pl.BlockSpec(memory_space=VMEM),
        scratch_shapes=[SMEM((TILES,), jnp.int32)],
        compiler_params=params(56),
        cost_estimate=pl.CostEstimate(flops=4 << 20, bytes_accessed=16 << 20, transcendentals=0),
        name="pack",
    )(dest, cell, velocity, mass, off, nor)


def weights_kernel(own_ref, source_ref, added_ref, *refs):
    halo, (inner_ref, outer_ref, diag_ref, first_ref, *faces) = refs[:6], refs[6:]
    own = own_ref[...] * ROOT
    columns = jnp.transpose(jnp.concatenate([own, jnp.zeros((80, 128), F32)], axis=0))
    total = jnp.zeros((128, 128), F32)
    inner, outer = list(enumerate(INNER)), list(enumerate(OUTER))
    for c in range(CELLS):
        mine = [columns[:, 16 * a + c : 16 * a + c + 1] for a in range(3)]
        rowsum = jnp.zeros((128, 128), F32)
        for index, (_, step, near) in [p for p in inner if p[1][0] == c]:
            square = None
            for a in range(3):
                gap = (own[16 * a + near : 16 * a + near + 1, :] + step[a] * ROOT) - mine[a]
                square = gap * gap if square is None else square + gap * gap
            weight = jnp.exp2(-square) * PER_PARTICLE
            inner_ref[index] = weight
            rowsum = rowsum + weight
        for index, (_, step, (which, row)) in [p for p in outer if p[1][0] == c]:
            count = 16 if which < 2 else 4
            square = None
            for a in range(3):
                at = count * a + row
                gap = (halo[which][at : at + 1, :] * ROOT + step[a] * ROOT) - mine[a]
                square = gap * gap if square is None else square + gap * gap
            weight = jnp.exp2(-square) * PER_PARTICLE
            outer_ref[index] = weight
            rowsum = rowsum + weight
        total = place_column(total, jnp.sum(rowsum, axis=1, keepdims=True), c)
    diag = jnp.transpose(total)[0:16, :] + (STIFFEN - PER_PARTICLE)
    diag_ref[...] = diag
    first = (source_ref[...] + added_ref[...]) / diag
    first_ref[...] = first
    write_faces(first, faces)


def weights(own, source, added, halo):
    outs = (shape(len(INNER), 128, 128), shape(len(OUTER), 128, 128), shape(16, 128), shape(16, 128))
    return pl.pallas_call(
        weights_kernel,
        out_shape=outs + (shape(4, 128),) * 4,
        in_specs=whole(9),
        out_specs=tuple(whole(8)),
        compiler_params=params(32),
        name="weights",
    )(own, source, added, *halo)


def inner_kernel(v_ref, w_ref, out_ref):
    total = jnp.zeros((128, 128), F32)
    for c in range(CELLS):
        product = None
        for index, (cell, _, near) in enumerate(INNER):
            if cell == c:
                term = w_ref[index] * v_ref[near : near + 1, :]
                product = term if product is None else product + term
        total = place_column(total, jnp.sum(product, axis=1, keepdims=True), c)
    out_ref[...] = jnp.transpose(total)[0:16, :]


def apply_inner(v, w):
    return pl.pallas_call(
        inner_kernel,
        out_shape=shape(16, 128),
        in_specs=whole(2),
        out_specs=pl.BlockSpec(memory_space=VMEM),
        compiler_params=params(16),
        cost_estimate=pl.CostEstimate(flops=4 << 20, bytes_accessed=5 << 20, transcendentals=0),
        name="apply_inner",
    )(v, w)


def outer_kernel(k, part_ref, diag_ref, w_ref, *refs):
    halo, basis, outs = refs[:6], refs[6 : 7 + k], refs[7 + k :]
    total = jnp.zeros((128, 128), F32)
    for c in range(CELLS):
        product = None
        for index, (cell, _, (which, row)) in enumerate(OUTER):
            if cell == c:
                term = w_ref[index] * halo[which][row : row + 1, :]
                product = term if product is None else product + term
        total = place_column(total, jnp.sum(product, axis=1, keepdims=True), c)
    image = jnp.transpose(total)[0:16, :] + part_ref[...]
    diag = diag_ref[...]
    v = basis[k][...]
    new = (image - PER_PARTICLE * v) / diag
    if SHIFT[k]:
        new = new - SHIFT[k] * v
    outs[0][...] = new
    if k < 3:
        write_faces(new, outs[1:5])
    else:
        vectors = [ref[...] for ref in basis] + [new]
        rows = []
        for i in range(4):
            scaled = vectors[i] * diag
            for j in range(i, 5):
                rows.append(jnp.sum(scaled * vectors[j], axis=0, keepdims=True))
        rows.append(jnp.zeros((128 - len(rows), 128), F32))
        lanes = jnp.sum(jnp.transpose(jnp.concatenate(rows, axis=0)), axis=0, keepdims=True)
        outs[1][...] = jnp.broadcast_to(lanes, (8, 128))


def apply_outer(k, part, diag, w, halo, basis):
    if k < 3:
        outs = (shape(16, 128),) + (shape(4, 128),) * 4
    else:
        outs = (shape(16, 128), shape(8, 128))
    return pl.pallas_call(
        functools.partial(outer_kernel, k),
        out_shape=outs,
        in_specs=whole(9 + k + 1),
        out_specs=tuple(whole(len(outs))),
        compiler_params=params(16),
        name="apply_outer",
    )(part, diag, w, *halo, *basis)


def coefficients(sums):
    table = {}
    lane = lax.broadcasted_iota(jnp.int32, (1, 128), 1)
    for index, (i, j) in enumerate(PAIRS):
        one = jnp.sum(jnp.where(lane == index, sums, 0.0), axis=1, keepdims=True)
        table[i, j] = table[j, i] = one
    scale, matrix = [], {}
    for i in range(4):
        for j in range(i + 1):
            one = (1.0 - SHIFT[j]) * table[i, j] - table[i, j + 1]
            if i != j:
                two = (1.0 - SHIFT[i]) * table[j, i] - table[j, i + 1]
                one = 0.5 * (one + two)
            matrix[i, j] = one
    for i in range(4):
        scale.append(lax.rsqrt(jnp.maximum(matrix[i, i], 1e-35)))
    right = [table[i, 0] * scale[i] for i in range(4)]
    lower, pivot = {}, []
    for j in range(4):
        value = matrix[j, j] * scale[j] * scale[j]
        for k in range(j):
            value = value - lower[j, k] * lower[j, k] * pivot[k]
        pivot.append(jnp.maximum(value, 3e-7))
        for i in range(j + 1, 4):
            value = matrix[i, j] * scale[i] * scale[j]
            for k in range(j):
                value = value - lower[i, k] * lower[j, k] * pivot[k]
            lower[i, j] = value / pivot[j]
    for i in range(4):
        for k in range(i):
            right[i] = right[i] - lower[i, k] * right[k]
    right = [right[i] / pivot[i] for i in range(4)]
    for i in reversed(range(4)):
        for k in range(i + 1, 4):
            right[i] = right[i] - lower[k, i] * right[k]
    return [right[i] * scale[i] for i in range(4)]


def advance(total, motion, mass, coefs, lanes):
    lane = lax.broadcasted_iota(jnp.int32, total.shape, 1)
    term = (lane >> 4) & 3
    factor = jnp.zeros(total.shape, F32)
    for k in range(4):
        factor = jnp.where(term == k, coefs[k], factor)
    scaled = jnp.where(lane < lanes, total * factor, 0.0)
    force = scaled
    for k in range(1, 4):
        force = force + pltpu.roll(scaled, 128 - 16 * k, 1)
    velocity = motion + STEP_TIME * force / mass
    moved = motion + STEP_TIME * pltpu.roll(velocity, 16, 1)
    kept = jnp.where(term == 0, velocity, jnp.where(term == 1, moved, 0.0))
    return jnp.where(lane < lanes, kept, 0.0)


def marker_kernel(step, *refs):
    if step == 0:
        codes_ref, recv_ref, feature_ref = refs[:3]
        n_ref, added_ref, rows_ref, moving_ref = refs[3:7]
        scratch = refs[7:]
    else:
        codes_ref, recv_ref, feature_ref, before_ref, diag_ref, payload_ref, motion_ref = refs[:7]
        basis = refs[7:12]
        n_ref, added_ref, first_ref, y0, y3, z0, z3, x_ref, moving_ref = refs[12:21]
        scratch = refs[21:]
    tile_ref, total_ref, even_ref, odd_ref = scratch

    if step == 0:
        moving_ref[0] = recv_ref[:, 49, :]
        moving_ref[1] = recv_ref[:, 50, :]
    else:
        coefs = coefficients(payload_ref[96:97, :])
        mass = recv_ref[:, 51, :]
        part = payload_ref[64:96, :]
        second = jnp.concatenate([part, pltpu.roll(part, 64, 1)], axis=0)
        moving_ref[0] = advance(payload_ref[0:64, :], motion_ref[0], mass, coefs, 128)
        moving_ref[1] = advance(second, motion_ref[1], mass, coefs, 64)

    row = lax.broadcasted_iota(jnp.int32, (8, 128), 0)
    lane = lax.broadcasted_iota(jnp.int32, (8, 128), 1)
    pick = jnp.where(row < 3, row * 4 + 1, jnp.where(row < 6, (row - 3) * 4, 32)) * 16
    scale = jnp.where(row < 3, ROOT, 1.0)

    def spread(s):
        low = jnp.broadcast_to(moving_ref[0, pl.ds(s, 1), :], (8, 128))
        high = jnp.broadcast_to(moving_ref[1, pl.ds(s, 1), :], (8, 128))
        tiles = []
        for r in range(8):
            target = pick + (codes_ref[s * 8 + r] >> 4)
            chosen = jnp.where(lane == target, low, jnp.where(lane + 128 == target, high, 0.0))
            tiles.append(jnp.broadcast_to(jnp.sum(chosen, axis=1, keepdims=True), (8, 128)) * scale)
        for r in range(8):
            tile_ref[s, r] = tiles[r]

    total_ref[...] = jnp.zeros((CELLS, 8, 128), F32)

    def weigh(s, r, buffer_ref):
        c = codes_ref[s * 8 + r] & 15
        place = recv_ref[s, 6 * r : 6 * r + 8, :] + tile_ref[s, r]
        high = place.astype(BF16).astype(F32)
        square = jnp.sum(jnp.where(row < 3, place * place, 0.0), axis=0, keepdims=True)
        square = jnp.broadcast_to(square, (8, 128))
        first = square.astype(BF16).astype(F32)
        second = (square - first).astype(BF16).astype(F32)
        third = square - first - second
        ends = jnp.where(row == 0, first, jnp.where(row == 1, second, jnp.where(row == 2, third, 1.0)))
        right = jnp.concatenate([high, place - high, high, ends], axis=0).astype(BF16)
        power = jnp.dot(feature_ref[c], right, preferred_element_type=F32)
        upper, lower = split2(jnp.exp2(power))
        buffer_ref[r, 0:128, :] = upper
        buffer_ref[r, 128:256, :] = lower

    def contract(s, r, buffer_ref):
        left = jnp.concatenate(split2(recv_ref[s, 6 * r : 6 * r + 8, :]), axis=0)
        both = lax.dot_general(left, buffer_ref[r], NT, preferred_element_type=F32)
        return both[0:8, 0:128] + both[8:16, 0:128] + both[0:8, 128:256]

    def turn(s_next, next_ref, s_now, now_ref):
        results = []
        for r in range(8):
            weigh(s_next, r, next_ref)
            results.append(contract(s_now, r, now_ref))
        for r in range(8):
            c = codes_ref[s_now * 8 + r] & 15
            total_ref[c] = total_ref[c] + results[r] * tile_ref[s_now, r]
            if r % 2 == 1:
                pair = pl.ds(pl.multiple_of(s_now * 32, 32) + 4 * (r - 1), 8)
                below, above = pltpu.roll(results[r - 1], 5, 0), pltpu.roll(results[r], 1, 0)
                n_ref[pair, :] = jnp.where(row < 4, below, above)
                if step == 0:
                    rows_ref[pair, :] = jnp.where(
                        row < 4, codes_ref[s_now * 8 + r - 1], codes_ref[s_now * 8 + r]
                    )
        spread(jnp.minimum(s_next + 1, TILES - 1))

    spread(0)
    for r in range(8):
        weigh(0, r, even_ref)
    spread(1)

    @pl.loop(0, TILES // 2)
    def _(t):
        turn(2 * t + 1, odd_ref, 2 * t, even_ref)
        turn(jnp.minimum(2 * t + 2, TILES - 1), even_ref, 2 * t + 1, odd_ref)

    for c in range(CELLS):
        added_ref[c : c + 1, :] = jnp.sum(total_ref[c][3:6, :], axis=0, keepdims=True)
    if step == 0:
        return
    vectors = [ref[...] for ref in basis]
    x = None
    first = vectors[0] + (added_ref[...] - before_ref[...]) / diag_ref[...]
    for k in range(4):
        term = coefs[k] * vectors[k]
        x = term if x is None else x + term
        first = first - coefs[k] * ((1.0 - SHIFT[k]) * vectors[k] - vectors[k + 1])
    x_ref[...] = x
    first_ref[...] = first
    write_faces(first, (y0, y3, z0, z3))


def marker_pass(step, *args):
    outs = (shape(4 * SLOTS, 128), shape(16, 128))
    if step:
        outs = outs + (shape(16, 128),) + (shape(4, 128),) * 4 + (shape(16, 128),)
    else:
        outs = outs + (shape(4 * SLOTS, 128, dtype=jnp.int32),)
    outs = outs + (shape(2, TILES, 128),)
    return pl.pallas_call(
        functools.partial(marker_kernel, step),
        out_shape=outs,
        in_specs=whole(1, SMEM) + whole(len(args) - 1),
        out_specs=tuple(whole(len(outs))),
        scratch_shapes=[
            VMEM((TILES, 8, 8, 128), F32),
            VMEM((CELLS, 8, 128), F32),
            VMEM((8, 256, 128), BF16),
            VMEM((8, 256, 128), BF16),
        ],
        compiler_params=params(32),
        name="markers",
    )(*args)


def features(own):
    def rounded(x):
        return lax.reduce_precision(x, 8, 7)

    o = (own.reshape(3, CELLS, 128) - 0.5) * ROOT
    high = rounded(2.0 * o)
    middle = rounded(2.0 * o - high)
    square = o[0] * o[0] + o[1] * o[1] + o[2] * o[2]
    first = rounded(square)
    second = rounded(square - first)
    third = square - first - second
    five, two = jnp.zeros((5, CELLS, 128), F32), jnp.zeros((2, CELLS, 128), F32)
    ends = jnp.concatenate([-jnp.ones((3, CELLS, 128), F32), -jnp.stack([first, second, third]), two])
    rows = jnp.concatenate([high, five, high, five, middle, five, ends])
    return jnp.transpose(rows, (1, 2, 0)).astype(BF16)


def force_kernel(n_ref, rows_ref, *refs):
    basis, out_ref, wide_ref = refs[:-2], refs[-2], refs[-1]
    count = len(basis)
    empty = jnp.zeros((16, 128), F32)
    vectors = [ref[...] for ref in basis]
    right_high, right_low = split2(jnp.concatenate(vectors + [empty] * (8 - count), axis=0))
    lane_cell = lax.broadcasted_iota(jnp.int32, (256, 128), 1) & 15
    source = lax.broadcasted_iota(jnp.int32, (128, 256), 0) >> 4
    target = lax.broadcasted_iota(jnp.int32, (128, 256), 1) >> 4
    spread = jnp.where((target % count == source) & (target < 3 * count), 1.0, 0.0).astype(BF16)
    lane = lax.broadcasted_iota(jnp.int32, (256, 256), 1)
    component = lax.broadcasted_iota(jnp.int32, (256, 256), 0) & 3
    fits = (lane >> 4) // count == component
    lane_grain = jnp.where(fits, lane & 15, -1)

    @pl.loop(0, 8)
    def _(chunk):
        rows = pl.ds(pl.multiple_of(chunk * 256, 256), 256)
        high, low = split2(n_ref[rows, :])
        dots = lax.dot_general(high, right_high, NT, preferred_element_type=F32)
        dots = dots + lax.dot_general(low, right_high, NT, preferred_element_type=F32)
        dots = dots + lax.dot_general(high, right_low, NT, preferred_element_type=F32)
        code = rows_ref[rows, :]
        dots = jnp.where(lane_cell == (code & 15), dots, 0.0)
        wide = None
        for piece in split3(dots):
            one = jnp.dot(piece, spread, preferred_element_type=F32)
            wide = one if wide is None else wide + one
        grain = jnp.concatenate([code, code], axis=1) >> 4
        kept = jnp.where(lane_grain == grain, wide, 0.0).reshape(8, 32, 256)
        wide_ref[pl.ds(pl.multiple_of(chunk * 8, 8), 8), :] = jnp.sum(kept, axis=1)

    if count == 4:
        out_ref[0:64, :] = wide_ref[:, 0:128]
        half = lax.broadcasted_iota(jnp.int32, (32, 128), 1) < 64
        below = pltpu.roll(wide_ref[32:64, 128:256], 64, 1)
        out_ref[64:96, :] = jnp.where(half, wide_ref[0:32, 128:256], below)
    else:
        out_ref[...] = wide_ref[...]


def forces(n, rows, basis):
    return pl.pallas_call(
        force_kernel,
        out_shape=shape(96, 128) if len(basis) == 4 else shape(64, 256),
        in_specs=whole(2 + len(basis)),
        out_specs=pl.BlockSpec(memory_space=VMEM),
        scratch_shapes=[VMEM((64, 256), F32)],
        compiler_params=params(32),
        cost_estimate=pl.CostEstimate(flops=4 << 20, bytes_accessed=16 << 20, transcendentals=0),
        name="forces",
    )(n, rows, *basis)


def final_kernel(got_ref, x_ref, *refs):
    basis, (out_ref, scaled_ref) = refs[:4], refs[4:]
    got = [jnp.sum(got_ref[:, h, :], axis=0, keepdims=True) for h in range(3)]
    coefs = coefficients(got[2])
    x = x_ref[...]
    for k in range(4):
        x = x + coefs[k] * basis[k][...]
    out_ref[...] = x
    for h in range(2):
        term = (lax.broadcasted_iota(jnp.int32, (1, 128), 1) // 16 + 8 * h) % 5
        factor = jnp.ones((1, 128), F32)
        for k in range(4):
            factor = jnp.where(term == k + 1, coefs[k], factor)
        scaled_ref[h : h + 1, :] = got[h] * factor


def final(got, x, basis):
    return pl.pallas_call(
        final_kernel,
        out_shape=(shape(16, 128), shape(2, 128)),
        in_specs=whole(6),
        out_specs=tuple(whole(2)),
        compiler_params=params(16),
        name="final",
    )(got, x, *basis)


def ring(x, axis, by):
    n = lax.axis_size(axis)
    return lax.ppermute(x, axis, [(i, (i + by) % n) for i in range(n)])


def halo_of(v, y0, y3, z0, z3):
    return (
        ring(v, "flow", -1),
        ring(v, "flow", 1),
        ring(y0, "cross", -1),
        ring(y3, "cross", 1),
        ring(z0, "depth", -1),
        ring(z3, "depth", 1),
    )


def exchange_sum(x, axes):
    for axis in axes:
        n = lax.axis_size(axis)
        m = 1
        while m < n:
            x = x + lax.ppermute(x, axis, [(i, i ^ m) for i in range(n)])
            m *= 2
    return x


def per_device(
    fluid_offsets,
    source,
    marker_offsets,
    marker_normals,
    dest_tile,
    cell_index,
    grain_velocity,
    grain_mass,
):
    source = source.reshape(16, 128)
    offs = fluid_offsets.reshape(3, 4, 4, 128)
    own = offs.reshape(48, 128)
    packed = pack(
        dest_tile.reshape(16, 16),
        cell_index,
        jnp.transpose(grain_velocity),
        grain_mass,
        jnp.transpose(marker_offsets, (0, 2, 1, 3)),
        jnp.transpose(marker_normals, (0, 2, 1, 3)),
    )
    recv = lax.all_to_all(packed, ("flow", "cross"), split_axis=0, concat_axis=0, tiled=True)
    halo = halo_of(
        own,
        offs[:, 0].reshape(12, 128),
        offs[:, 3].reshape(12, 128),
        offs[:, :, 0].reshape(12, 128),
        offs[:, :, 3].reshape(12, 128),
    )
    feature = features(own)
    codes = recv[:, 48, 0:8].astype(jnp.int32).reshape(SLOTS)

    x = None
    n = rows = motion = added = basis = payload = None
    for step in range(STEPS):
        if step == 0:
            n, added, rows, motion = marker_pass(0, codes, recv, feature)
            w_inner, w_outer, diag, v, *faces = weights(own, source, added, halo)
        else:
            n, added, v, *rest = marker_pass(
                1, codes, recv, feature, added, diag, payload, motion, *basis
            )
            faces, x, motion = rest[:4], rest[4], rest[5]
        basis = [v]
        for k in range(4):
            halo = halo_of(basis[k], *faces)
            part = apply_inner(basis[k], w_inner)
            if k == 3:
                felt = forces(n, rows, ([x] if step else []) + basis)
                part, felt = lax.optimization_barrier((part, felt))
            v, *faces = apply_outer(k, part, diag, w_outer, halo, basis)
            basis.append(v)
        sums = sum([ring(faces[0], "depth", by) for by in range(1, lax.axis_size("depth"))], faces[0])
        if step < STEPS - 1:
            payload = exchange_sum(jnp.concatenate([felt, sums]), ("flow", "cross"))
    send = jnp.concatenate([felt.reshape(TILES, 2, 128), jnp.broadcast_to(sums[0:1], (TILES, 1, 128))], axis=1)
    got = lax.all_to_all(send, ("flow", "cross"), split_axis=0, concat_axis=0, tiled=True)
    pressure, scaled = final(got, x, basis[:4])
    force = jnp.sum(scaled.reshape(256)[:240].reshape(3, 5, 16), axis=1)
    index = lax.axis_index("flow") * lax.axis_size("cross") + lax.axis_index("cross")
    mine = lax.dynamic_slice_in_dim(motion, index, 1, axis=1).reshape(4, 64)[:3, :16]
    velocity = jnp.transpose(mine + STEP_TIME * force / grain_mass[None, :])
    return pressure.reshape(1, 4, 4, 128), velocity


def solution(mesh):
    owners = ("flow", "cross", "depth")
    return jax.shard_map(
        per_device,
        mesh=mesh,
        in_specs=(
            P(None, "flow", "cross", "depth", None),
            P("flow", "cross", "depth", None),
            P(owners, None, None, None),
            P(owners, None, None, None),
            P(owners, None, None),
            P(owners, None),
            P(owners, None),
            P(owners),
        ),
        out_specs=(P("flow", "cross", "depth", None), P(owners, None)),
        check_vma=False,
    )
```

```python
import functools

import jax
import jax.numpy as jnp
from jax import lax
from jax.experimental import pallas as pl
from jax.experimental.pallas import tpu as pltpu
from jax.sharding import PartitionSpec as P

STEPS = 2
STIFFEN = 0.5
STEP_TIME = 0.05
PER_PARTICLE = 1.0 / 128.0
ROOT = 1.2011224087864498
SHIFT = (0.0, 0.7, 0.3, 0.5)
CELLS = 16
SLOTS = 512
TILES = 64
CAP = 8
F32 = jnp.float32
BF16 = jnp.bfloat16
VMEM = pltpu.VMEM
SMEM = pltpu.SMEM
NT = (((1,), (1,)), ((), ()))
PAIRS = tuple((i, j) for i in range(4) for j in range(i, 5))


def params(mib):
    return pltpu.CompilerParams(vmem_limit_bytes=mib * 1024 * 1024)


def whole(count, space=VMEM):
    return [pl.BlockSpec(memory_space=space)] * count


def shape(*dims, dtype=F32):
    return jax.ShapeDtypeStruct(dims, dtype)


def inner_pairs():
    out = []
    for c in range(CELLS):
        y, z = c // 4, c % 4
        out.append((c, (0, 0, 0), c))
        if y < 3:
            out.append((c, (0, 1, 0), c + 4))
        if y > 0:
            out.append((c, (0, -1, 0), c - 4))
        if z < 3:
            out.append((c, (0, 0, 1), c + 1))
        if z > 0:
            out.append((c, (0, 0, -1), c - 1))
    return out


def outer_pairs():
    out = []
    for c in range(CELLS):
        y, z = c // 4, c % 4
        out.append((c, (1, 0, 0), (0, c)))
        out.append((c, (-1, 0, 0), (1, c)))
        if y == 3:
            out.append((c, (0, 1, 0), (2, z)))
        if y == 0:
            out.append((c, (0, -1, 0), (3, z)))
        if z == 3:
            out.append((c, (0, 0, 1), (4, y)))
        if z == 0:
            out.append((c, (0, 0, -1), (5, y)))
    return out


INNER = inner_pairs()
OUTER = outer_pairs()


def split2(x):
    high = x.astype(BF16)
    return high, (x - high.astype(F32)).astype(BF16)


def split3(x):
    high = x.astype(BF16)
    rest = x - high.astype(F32)
    middle = rest.astype(BF16)
    return high, middle, (rest - middle.astype(F32)).astype(BF16)


def place_column(total, column, c):
    lane = lax.broadcasted_iota(jnp.int32, (128, 128), 1)
    return jnp.where(lane == c, column, total)


def write_faces(v, faces):
    y0, y3, z0, z3 = faces
    y0[...] = v[0:4, :]
    y3[...] = v[12:16, :]
    for y in range(4):
        z0[y : y + 1, :] = v[4 * y : 4 * y + 1, :]
        z3[y : y + 1, :] = v[4 * y + 3 : 4 * y + 4, :]


def pack_kernel(dest_ref, cell_ref, velocity_ref, mass_ref, off_ref, nor_ref, buf_ref, count_ref):
    buf_ref[:, 0:48, :] = jnp.zeros((TILES, 48, 128), F32)
    row = lax.broadcasted_iota(jnp.int32, (8, 128), 0)
    place = lax.broadcasted_iota(jnp.int32, (8, 128), 1)
    meta = jnp.zeros((8, 128), F32)
    for g in range(16):
        for a in range(3):
            here = (row == 1 + a // 2) & (place == 64 * (a % 2) + g)
            meta = jnp.where(here, velocity_ref[a, g], meta)
        meta = jnp.where((row == 3) & ((place & 15) == g), mass_ref[g], meta)

    @pl.loop(0, TILES)
    def _(t):
        buf_ref[t, 48:56, :] = meta
        count_ref[t] = 0

    lane = lax.broadcasted_iota(jnp.int32, (1, 128), 1)

    @pl.loop(0, 16)
    def _(g):
        off = [(off_ref[g, a] - 0.5) * ROOT for a in range(3)]
        nor = [nor_ref[g, a] * PER_PARTICLE for a in range(3)]
        for b in range(16):
            d = dest_ref[g, b]
            r = count_ref[d]
            count_ref[d] = r + 1
            for a in range(3):
                buf_ref[d, pl.ds(6 * r + a, 1), :] = off[a][b : b + 1, :]
                buf_ref[d, pl.ds(6 * r + 3 + a, 1), :] = nor[a][b : b + 1, :]
            code = (cell_ref[g, b] + 16 * g).astype(F32)
            buf_ref[d, 48:49, :] = jnp.where(lane == r, code, buf_ref[d, 48:49, :])


def pack(dest, cell, velocity, mass, off, nor):
    return pl.pallas_call(
        pack_kernel,
        out_shape=shape(TILES, 56, 128),
        in_specs=whole(4, SMEM) + whole(2),
        out_specs=pl.BlockSpec(memory_space=VMEM),
        scratch_shapes=[SMEM((TILES,), jnp.int32)],
        compiler_params=params(56),
        cost_estimate=pl.CostEstimate(flops=4 << 20, bytes_accessed=16 << 20, transcendentals=0),
        name="pack",
    )(dest, cell, velocity, mass, off, nor)


def weights_kernel(own_ref, source_ref, added_ref, *refs):
    halo, (inner_ref, outer_ref, diag_ref, first_ref, *faces) = refs[:6], refs[6:]
    own = own_ref[...] * ROOT
    columns = jnp.transpose(jnp.concatenate([own, jnp.zeros((80, 128), F32)], axis=0))
    total = jnp.zeros((128, 128), F32)
    inner, outer = list(enumerate(INNER)), list(enumerate(OUTER))
    for c in range(CELLS):
        mine = [columns[:, 16 * a + c : 16 * a + c + 1] for a in range(3)]
        rowsum = jnp.zeros((128, 128), F32)
        for index, (_, step, near) in [p for p in inner if p[1][0] == c]:
            square = None
            for a in range(3):
                gap = (own[16 * a + near : 16 * a + near + 1, :] + step[a] * ROOT) - mine[a]
                square = gap * gap if square is None else square + gap * gap
            weight = jnp.exp2(-square) * PER_PARTICLE
            inner_ref[index] = weight
            rowsum = rowsum + weight
        for index, (_, step, (which, row)) in [p for p in outer if p[1][0] == c]:
            count = 16 if which < 2 else 4
            square = None
            for a in range(3):
                at = count * a + row
                gap = (halo[which][at : at + 1, :] * ROOT + step[a] * ROOT) - mine[a]
                square = gap * gap if square is None else square + gap * gap
            weight = jnp.exp2(-square) * PER_PARTICLE
            outer_ref[index] = weight
            rowsum = rowsum + weight
        total = place_column(total, jnp.sum(rowsum, axis=1, keepdims=True), c)
    diag = jnp.transpose(total)[0:16, :] + (STIFFEN - PER_PARTICLE)
    diag_ref[...] = diag
    first = (source_ref[...] + added_ref[...]) / diag
    first_ref[...] = first
    write_faces(first, faces)


def weights(own, source, added, halo):
    outs = (shape(len(INNER), 128, 128), shape(len(OUTER), 128, 128), shape(16, 128), shape(16, 128))
    return pl.pallas_call(
        weights_kernel,
        out_shape=outs + (shape(4, 128),) * 4,
        in_specs=whole(9),
        out_specs=tuple(whole(8)),
        compiler_params=params(32),
        name="weights",
    )(own, source, added, *halo)


def inner_kernel(v_ref, w_ref, out_ref):
    total = jnp.zeros((128, 128), F32)
    for c in range(CELLS):
        product = None
        for index, (cell, _, near) in enumerate(INNER):
            if cell == c:
                term = w_ref[index] * v_ref[near : near + 1, :]
                product = term if product is None else product + term
        total = place_column(total, jnp.sum(product, axis=1, keepdims=True), c)
    out_ref[...] = jnp.transpose(total)[0:16, :]


def apply_inner(v, w):
    return pl.pallas_call(
        inner_kernel,
        out_shape=shape(16, 128),
        in_specs=whole(2),
        out_specs=pl.BlockSpec(memory_space=VMEM),
        compiler_params=params(16),
        cost_estimate=pl.CostEstimate(flops=4 << 20, bytes_accessed=5 << 20, transcendentals=0),
        name="apply_inner",
    )(v, w)


def outer_kernel(k, part_ref, diag_ref, w_ref, *refs):
    halo, basis, outs = refs[:6], refs[6 : 7 + k], refs[7 + k :]
    total = jnp.zeros((128, 128), F32)
    for c in range(CELLS):
        product = None
        for index, (cell, _, (which, row)) in enumerate(OUTER):
            if cell == c:
                term = w_ref[index] * halo[which][row : row + 1, :]
                product = term if product is None else product + term
        total = place_column(total, jnp.sum(product, axis=1, keepdims=True), c)
    image = jnp.transpose(total)[0:16, :] + part_ref[...]
    diag = diag_ref[...]
    v = basis[k][...]
    new = (image - PER_PARTICLE * v) / diag
    if SHIFT[k]:
        new = new - SHIFT[k] * v
    outs[0][...] = new
    if k < 3:
        write_faces(new, outs[1:5])
    else:
        vectors = [ref[...] for ref in basis] + [new]
        rows = []
        for i in range(4):
            scaled = vectors[i] * diag
            for j in range(i, 5):
                rows.append(jnp.sum(scaled * vectors[j], axis=0, keepdims=True))
        rows.append(jnp.zeros((128 - len(rows), 128), F32))
        lanes = jnp.sum(jnp.transpose(jnp.concatenate(rows, axis=0)), axis=0, keepdims=True)
        outs[1][...] = jnp.broadcast_to(lanes, (8, 128))


def apply_outer(k, part, diag, w, halo, basis):
    if k < 3:
        outs = (shape(16, 128),) + (shape(4, 128),) * 4
    else:
        outs = (shape(16, 128), shape(8, 128))
    return pl.pallas_call(
        functools.partial(outer_kernel, k),
        out_shape=outs,
        in_specs=whole(9 + k + 1),
        out_specs=tuple(whole(len(outs))),
        compiler_params=params(16),
        name="apply_outer",
    )(part, diag, w, *halo, *basis)


def coefficients(sums):
    table = {}
    lane = lax.broadcasted_iota(jnp.int32, (1, 128), 1)
    for index, (i, j) in enumerate(PAIRS):
        one = jnp.sum(jnp.where(lane == index, sums, 0.0), axis=1, keepdims=True)
        table[i, j] = table[j, i] = one
    scale, matrix = [], {}
    for i in range(4):
        for j in range(i + 1):
            one = (1.0 - SHIFT[j]) * table[i, j] - table[i, j + 1]
            if i != j:
                two = (1.0 - SHIFT[i]) * table[j, i] - table[j, i + 1]
                one = 0.5 * (one + two)
            matrix[i, j] = one
    for i in range(4):
        scale.append(lax.rsqrt(jnp.maximum(matrix[i, i], 1e-35)))
    right = [table[i, 0] * scale[i] for i in range(4)]
    lower, pivot = {}, []
    for j in range(4):
        value = matrix[j, j] * scale[j] * scale[j]
        for k in range(j):
            value = value - lower[j, k] * lower[j, k] * pivot[k]
        pivot.append(jnp.maximum(value, 3e-7))
        for i in range(j + 1, 4):
            value = matrix[i, j] * scale[i] * scale[j]
            for k in range(j):
                value = value - lower[i, k] * lower[j, k] * pivot[k]
            lower[i, j] = value / pivot[j]
    for i in range(4):
        for k in range(i):
            right[i] = right[i] - lower[i, k] * right[k]
    right = [right[i] / pivot[i] for i in range(4)]
    for i in reversed(range(4)):
        for k in range(i + 1, 4):
            right[i] = right[i] - lower[k, i] * right[k]
    return [right[i] * scale[i] for i in range(4)]


def advance(total, motion, mass, coefs, lanes):
    lane = lax.broadcasted_iota(jnp.int32, total.shape, 1)
    term = (lane >> 4) & 3
    factor = jnp.zeros(total.shape, F32)
    for k in range(4):
        factor = jnp.where(term == k, coefs[k], factor)
    scaled = jnp.where(lane < lanes, total * factor, 0.0)
    force = scaled
    for k in range(1, 4):
        force = force + pltpu.roll(scaled, 128 - 16 * k, 1)
    velocity = motion + STEP_TIME * force / mass
    moved = motion + STEP_TIME * pltpu.roll(velocity, 16, 1)
    kept = jnp.where(term == 0, velocity, jnp.where(term == 1, moved, 0.0))
    return jnp.where(lane < lanes, kept, 0.0)


def marker_kernel(step, *refs):
    if step == 0:
        codes_ref, recv_ref, feature_ref = refs[:3]
        n_ref, added_ref, rows_ref, moving_ref = refs[3:7]
        scratch = refs[7:]
    else:
        codes_ref, recv_ref, feature_ref, before_ref, diag_ref, payload_ref, motion_ref = refs[:7]
        basis = refs[7:12]
        n_ref, added_ref, first_ref, y0, y3, z0, z3, x_ref, moving_ref = refs[12:21]
        scratch = refs[21:]
    tile_ref, total_ref, even_ref, odd_ref = scratch

    if step == 0:
        moving_ref[0] = recv_ref[:, 49, :]
        moving_ref[1] = recv_ref[:, 50, :]
    else:
        coefs = coefficients(payload_ref[96:97, :])
        mass = recv_ref[:, 51, :]
        part = payload_ref[64:96, :]
        second = jnp.concatenate([part, pltpu.roll(part, 64, 1)], axis=0)
        moving_ref[0] = advance(payload_ref[0:64, :], motion_ref[0], mass, coefs, 128)
        moving_ref[1] = advance(second, motion_ref[1], mass, coefs, 64)

    row = lax.broadcasted_iota(jnp.int32, (8, 128), 0)
    lane = lax.broadcasted_iota(jnp.int32, (8, 128), 1)
    pick = jnp.where(row < 3, row * 4 + 1, jnp.where(row < 6, (row - 3) * 4, 32)) * 16
    scale = jnp.where(row < 3, ROOT, 1.0)

    def spread(s):
        low = jnp.broadcast_to(moving_ref[0, pl.ds(s, 1), :], (8, 128))
        high = jnp.broadcast_to(moving_ref[1, pl.ds(s, 1), :], (8, 128))
        tiles = []
        for r in range(8):
            target = pick + (codes_ref[s * 8 + r] >> 4)
            chosen = jnp.where(lane == target, low, jnp.where(lane + 128 == target, high, 0.0))
            tiles.append(jnp.broadcast_to(jnp.sum(chosen, axis=1, keepdims=True), (8, 128)) * scale)
        for r in range(8):
            tile_ref[s, r] = tiles[r]

    total_ref[...] = jnp.zeros((CELLS, 8, 128), F32)

    def weigh(s, r, buffer_ref):
        c = codes_ref[s * 8 + r] & 15
        place = recv_ref[s, 6 * r : 6 * r + 8, :] + tile_ref[s, r]
        high = place.astype(BF16).astype(F32)
        square = jnp.sum(jnp.where(row < 3, place * place, 0.0), axis=0, keepdims=True)
        square = jnp.broadcast_to(square, (8, 128))
        first = square.astype(BF16).astype(F32)
        second = (square - first).astype(BF16).astype(F32)
        third = square - first - second
        ends = jnp.where(row == 0, first, jnp.where(row == 1, second, jnp.where(row == 2, third, 1.0)))
        right = jnp.concatenate([high, place - high, high, ends], axis=0).astype(BF16)
        power = jnp.dot(feature_ref[c], right, preferred_element_type=F32)
        upper, lower = split2(jnp.exp2(power))
        buffer_ref[r, 0:128, :] = upper
        buffer_ref[r, 128:256, :] = lower

    def contract(s, r, buffer_ref):
        left = jnp.concatenate(split2(recv_ref[s, 6 * r : 6 * r + 8, :]), axis=0)
        both = lax.dot_general(left, buffer_ref[r], NT, preferred_element_type=F32)
        return both[0:8, 0:128] + both[8:16, 0:128] + both[0:8, 128:256]

    def turn(s_next, next_ref, s_now, now_ref):
        results = []
        for r in range(8):
            weigh(s_next, r, next_ref)
            results.append(contract(s_now, r, now_ref))
        for r in range(8):
            c = codes_ref[s_now * 8 + r] & 15
            total_ref[c] = total_ref[c] + results[r] * tile_ref[s_now, r]
            if r % 2 == 1:
                pair = pl.ds(pl.multiple_of(s_now * 32, 32) + 4 * (r - 1), 8)
                below, above = pltpu.roll(results[r - 1], 5, 0), pltpu.roll(results[r], 1, 0)
                n_ref[pair, :] = jnp.where(row < 4, below, above)
                if step == 0:
                    rows_ref[pair, :] = jnp.where(
                        row < 4, codes_ref[s_now * 8 + r - 1], codes_ref[s_now * 8 + r]
                    )
        spread(jnp.minimum(s_next + 1, TILES - 1))

    spread(0)
    for r in range(8):
        weigh(0, r, even_ref)
    spread(1)

    @pl.loop(0, TILES // 2)
    def _(t):
        turn(2 * t + 1, odd_ref, 2 * t, even_ref)
        turn(jnp.minimum(2 * t + 2, TILES - 1), even_ref, 2 * t + 1, odd_ref)

    for c in range(CELLS):
        added_ref[c : c + 1, :] = jnp.sum(total_ref[c][3:6, :], axis=0, keepdims=True)
    if step == 0:
        return
    vectors = [ref[...] for ref in basis]
    x = None
    first = vectors[0] + (added_ref[...] - before_ref[...]) / diag_ref[...]
    for k in range(4):
        term = coefs[k] * vectors[k]
        x = term if x is None else x + term
        first = first - coefs[k] * ((1.0 - SHIFT[k]) * vectors[k] - vectors[k + 1])
    x_ref[...] = x
    first_ref[...] = first
    write_faces(first, (y0, y3, z0, z3))


def marker_pass(step, *args):
    outs = (shape(4 * SLOTS, 128), shape(16, 128))
    if step:
        outs = outs + (shape(16, 128),) + (shape(4, 128),) * 4 + (shape(16, 128),)
    else:
        outs = outs + (shape(4 * SLOTS, 128, dtype=jnp.int32),)
    outs = outs + (shape(2, TILES, 128),)
    return pl.pallas_call(
        functools.partial(marker_kernel, step),
        out_shape=outs,
        in_specs=whole(1, SMEM) + whole(len(args) - 1),
        out_specs=tuple(whole(len(outs))),
        scratch_shapes=[
            VMEM((TILES, 8, 8, 128), F32),
            VMEM((CELLS, 8, 128), F32),
            VMEM((8, 256, 128), BF16),
            VMEM((8, 256, 128), BF16),
        ],
        compiler_params=params(32),
        name="markers",
    )(*args)


def features(own):
    def rounded(x):
        return lax.reduce_precision(x, 8, 7)

    o = (own.reshape(3, CELLS, 128) - 0.5) * ROOT
    high = rounded(2.0 * o)
    middle = rounded(2.0 * o - high)
    square = o[0] * o[0] + o[1] * o[1] + o[2] * o[2]
    first = rounded(square)
    second = rounded(square - first)
    third = square - first - second
    five, two = jnp.zeros((5, CELLS, 128), F32), jnp.zeros((2, CELLS, 128), F32)
    ends = jnp.concatenate([-jnp.ones((3, CELLS, 128), F32), -jnp.stack([first, second, third]), two])
    rows = jnp.concatenate([high, five, high, five, middle, five, ends])
    return jnp.transpose(rows, (1, 2, 0)).astype(BF16)


def force_kernel(n_ref, rows_ref, *refs):
    basis, out_ref, wide_ref = refs[:-2], refs[-2], refs[-1]
    count = len(basis)
    empty = jnp.zeros((16, 128), F32)
    vectors = [ref[...] for ref in basis]
    right_high, right_low = split2(jnp.concatenate(vectors + [empty] * (8 - count), axis=0))
    lane_cell = lax.broadcasted_iota(jnp.int32, (256, 128), 1) & 15
    source = lax.broadcasted_iota(jnp.int32, (128, 256), 0) >> 4
    target = lax.broadcasted_iota(jnp.int32, (128, 256), 1) >> 4
    spread = jnp.where((target % count == source) & (target < 3 * count), 1.0, 0.0).astype(BF16)
    lane = lax.broadcasted_iota(jnp.int32, (256, 256), 1)
    component = lax.broadcasted_iota(jnp.int32, (256, 256), 0) & 3
    fits = (lane >> 4) // count == component
    lane_grain = jnp.where(fits, lane & 15, -1)

    @pl.loop(0, 8)
    def _(chunk):
        rows = pl.ds(pl.multiple_of(chunk * 256, 256), 256)
        high, low = split2(n_ref[rows, :])
        dots = lax.dot_general(high, right_high, NT, preferred_element_type=F32)
        dots = dots + lax.dot_general(low, right_high, NT, preferred_element_type=F32)
        dots = dots + lax.dot_general(high, right_low, NT, preferred_element_type=F32)
        code = rows_ref[rows, :]
        dots = jnp.where(lane_cell == (code & 15), dots, 0.0)
        wide = None
        for piece in split3(dots):
            one = jnp.dot(piece, spread, preferred_element_type=F32)
            wide = one if wide is None else wide + one
        grain = jnp.concatenate([code, code], axis=1) >> 4
        kept = jnp.where(lane_grain == grain, wide, 0.0).reshape(8, 32, 256)
        wide_ref[pl.ds(pl.multiple_of(chunk * 8, 8), 8), :] = jnp.sum(kept, axis=1)

    if count == 4:
        out_ref[0:64, :] = wide_ref[:, 0:128]
        half = lax.broadcasted_iota(jnp.int32, (32, 128), 1) < 64
        below = pltpu.roll(wide_ref[32:64, 128:256], 64, 1)
        out_ref[64:96, :] = jnp.where(half, wide_ref[0:32, 128:256], below)
    else:
        out_ref[...] = wide_ref[...]


def forces(n, rows, basis):
    return pl.pallas_call(
        force_kernel,
        out_shape=shape(96, 128) if len(basis) == 4 else shape(64, 256),
        in_specs=whole(2 + len(basis)),
        out_specs=pl.BlockSpec(memory_space=VMEM),
        scratch_shapes=[VMEM((64, 256), F32)],
        compiler_params=params(32),
        cost_estimate=pl.CostEstimate(flops=4 << 20, bytes_accessed=16 << 20, transcendentals=0),
        name="forces",
    )(n, rows, *basis)


def final_kernel(got_ref, x_ref, *refs):
    basis, (out_ref, scaled_ref) = refs[:4], refs[4:]
    got = [jnp.sum(got_ref[:, h, :], axis=0, keepdims=True) for h in range(3)]
    coefs = coefficients(got[2])
    x = x_ref[...]
    for k in range(4):
        x = x + coefs[k] * basis[k][...]
    out_ref[...] = x
    for h in range(2):
        term = (lax.broadcasted_iota(jnp.int32, (1, 128), 1) // 16 + 8 * h) % 5
        factor = jnp.ones((1, 128), F32)
        for k in range(4):
            factor = jnp.where(term == k + 1, coefs[k], factor)
        scaled_ref[h : h + 1, :] = got[h] * factor


def final(got, x, basis):
    return pl.pallas_call(
        final_kernel,
        out_shape=(shape(16, 128), shape(2, 128)),
        in_specs=whole(6),
        out_specs=tuple(whole(2)),
        compiler_params=params(16),
        name="final",
    )(got, x, *basis)


def ring(x, axis, by):
    n = lax.axis_size(axis)
    return lax.ppermute(x, axis, [(i, (i + by) % n) for i in range(n)])


def both_sides(first, last, axis):
    n = lax.axis_size(axis)
    even = lax.axis_index(axis) % 2 == 0
    same = first is last
    inside = lax.ppermute(
        first if same else jnp.where(even, last, first), axis, [(i, i ^ 1) for i in range(n)]
    )
    across = lax.ppermute(
        first if same else jnp.where(even, first, last),
        axis,
        [(i, (i + (1 if i % 2 else -1)) % n) for i in range(n)],
    )
    return jnp.where(even, inside, across), jnp.where(even, across, inside)


def halo_of(v, y0, y3, z0, z3):
    return (
        both_sides(v, v, "flow") + both_sides(y0, y3, "cross") + both_sides(z0, z3, "depth")
    )


def exchange_sum(x, axes):
    for axis in axes:
        n = lax.axis_size(axis)
        m = 1
        while m < n:
            x = x + lax.ppermute(x, axis, [(i, i ^ m) for i in range(n)])
            m *= 2
    return x


def per_device(
    fluid_offsets,
    source,
    marker_offsets,
    marker_normals,
    dest_tile,
    cell_index,
    grain_velocity,
    grain_mass,
):
    source = source.reshape(16, 128)
    offs = fluid_offsets.reshape(3, 4, 4, 128)
    own = offs.reshape(48, 128)
    packed = pack(
        dest_tile.reshape(16, 16),
        cell_index,
        jnp.transpose(grain_velocity),
        grain_mass,
        jnp.transpose(marker_offsets, (0, 2, 1, 3)),
        jnp.transpose(marker_normals, (0, 2, 1, 3)),
    )
    recv = lax.all_to_all(packed, ("flow", "cross"), split_axis=0, concat_axis=0, tiled=True)
    halo = halo_of(
        own,
        offs[:, 0].reshape(12, 128),
        offs[:, 3].reshape(12, 128),
        offs[:, :, 0].reshape(12, 128),
        offs[:, :, 3].reshape(12, 128),
    )
    feature = features(own)
    codes = recv[:, 48, 0:8].astype(jnp.int32).reshape(SLOTS)

    x = None
    n = rows = motion = added = basis = payload = None
    for step in range(STEPS):
        if step == 0:
            n, added, rows, motion = marker_pass(0, codes, recv, feature)
            w_inner, w_outer, diag, v, *faces = weights(own, source, added, halo)
        else:
            n, added, v, *rest = marker_pass(
                1, codes, recv, feature, added, diag, payload, motion, *basis
            )
            faces, x, motion = rest[:4], rest[4], rest[5]
        basis = [v]
        for k in range(4):
            halo = halo_of(basis[k], *faces)
            part = apply_inner(basis[k], w_inner)
            v, *faces = apply_outer(k, part, diag, w_outer, halo, basis)
            basis.append(v)
        sums = sum([ring(faces[0], "depth", by) for by in range(1, lax.axis_size("depth"))], faces[0])
        if step < STEPS - 1:
            felt = forces(n, rows, basis[:4])
            payload = exchange_sum(jnp.concatenate([felt, sums]), ("flow", "cross"))
    felt = forces(n, rows, [x] + basis[:4]).reshape(TILES, 2, 128)
    send = jnp.concatenate([felt, jnp.broadcast_to(sums[0:1], (TILES, 1, 128))], axis=1)
    got = lax.all_to_all(send, ("flow", "cross"), split_axis=0, concat_axis=0, tiled=True)
    pressure, scaled = final(got, x, basis[:4])
    force = jnp.sum(scaled.reshape(256)[:240].reshape(3, 5, 16), axis=1)
    index = lax.axis_index("flow") * lax.axis_size("cross") + lax.axis_index("cross")
    mine = lax.dynamic_slice_in_dim(motion, index, 1, axis=1).reshape(4, 64)[:3, :16]
    velocity = jnp.transpose(mine + STEP_TIME * force / grain_mass[None, :])
    return pressure.reshape(1, 4, 4, 128), velocity


def solution(mesh):
    owners = ("flow", "cross", "depth")
    return jax.shard_map(
        per_device,
        mesh=mesh,
        in_specs=(
            P(None, "flow", "cross", "depth", None),
            P("flow", "cross", "depth", None),
            P(owners, None, None, None),
            P(owners, None, None, None),
            P(owners, None, None),
            P(owners, None),
            P(owners, None),
            P(owners),
        ),
        out_specs=(P("flow", "cross", "depth", None), P(owners, None)),
        check_vma=False,
    )
```
